512 devices in a mesh: chain: 8 (over y), sector: 16 (over z, core), term: 4 (over x).
Axes of the slice: x: 4, y: 8, z: 8, core: 2. Of those that a mesh axis runs over, the one named last changes fastest.
Arguments:
- two_site: float32 [8, 16, 256, 256], P('chain', 'sector'), may hold values from -6 to 6
- left_env: bfloat16 [8, 40, 16, 256, 256], P('chain', 'term', 'sector'), may hold values from -1 to 2
- right_env: bfloat16 [8, 40, 16, 256, 256], P('chain', 'term', 'sector'), may hold values from -1 to 2
- block_dims: int32 [16], P('sector'), may hold values from 128 to 256, as said below
- sources: int32 [40, 16, 3], P('term', 'sector'), may hold values from 0 to 15, as said below
- sixj_index: int32 [40, 16, 3], P('term', 'sector'), may hold values from 0 to 63, as said below
- sixj_table: float32 [64], replicated, may hold values from -1 to 1
Outputs:
- solution: bfloat16 [8, 16, 256, 256], P('chain', 'sector')
- energy: float32 [8], P('chain')
- handoff: bfloat16 [8, 40, 16, 256, 256], P('chain', 'term', 'sector')
The draws below stay inside these ranges and needn't reach their ends.
Inputs may be any that keep to these rules, and one draw needn't show every extreme that they name: `block_dims`: at least one sector block has dimension 256. sources[w, b, 0] = b for every term w and sector b. sixj_index[w, b, 0] < 16 for every term w and sector b.
All inputs are finite; a program needn't handle non-finite values.
Results may differ from the reference program's by a relative error of at most 0.03.
Values may be sent and summed in bfloat16 or wider, within the bound.
A program may use at most 64 MiB of HBM per device.

```python
import math
import jax
import jax.numpy as jnp
from jax import lax

M = 256
ITERS = 4
K = 3
TABLE = 64
SEGS = 8
SECTORS = 16
TERMS = 40


def draw_block_dims(key, part):
    first_key, second_key = jax.random.split(jax.random.fold_in(key, 7))
    values = jax.random.randint(first_key, (SECTORS,), M // 2, M + 1)
    chosen = jax.random.randint(second_key, (), 0, SECTORS)
    return jnp.where(jnp.arange(SECTORS) == chosen, M, values).astype(jnp.int32)


def environment(key, salt, diag_low, diag_high):
    noise_key, scale_key, diag_key = jax.random.split(jax.random.fold_in(key, salt), 3)
    shape = (SEGS, TERMS, SECTORS, M, M)
    spread = 0.8 / math.sqrt(M)
    noise = jnp.clip(jax.random.normal(noise_key, shape, jnp.float32), -4.0, 4.0) * spread
    block_scale = jnp.exp(jax.random.uniform(scale_key, (SEGS, TERMS, SECTORS, 1, 1), jnp.float32, math.log(0.5), math.log(2.0)))
    diag_values = jnp.exp(jax.random.uniform(diag_key, (SEGS, TERMS, SECTORS, M, 1), jnp.float32, math.log(diag_low), math.log(diag_high)))
    rows = jnp.arange(M, dtype=jnp.int32)
    identity = (rows[:, None] == rows[None, :]).astype(jnp.float32)
    return (noise + identity * block_scale * diag_values).astype(jnp.bfloat16)


def draw_left_env(key, part):
    return environment(key, 11, 0.1, 0.4)


def draw_right_env(key, part):
    return environment(key, 13, 0.2, 0.8)


def draw_sources(key, part):
    picked = jax.random.randint(jax.random.fold_in(key, 17), (TERMS, SECTORS, K), 0, SECTORS)
    own = jnp.broadcast_to(jnp.arange(SECTORS, dtype=jnp.int32)[None, :, None], (TERMS, SECTORS, K))
    slot = jnp.arange(K, dtype=jnp.int32)[None, None, :]
    return jnp.where(slot == 0, own, picked).astype(jnp.int32)


def draw_sixj_index(key, part):
    low_key, high_key, term_key = jax.random.split(jax.random.fold_in(key, 19), 3)
    low = jax.random.randint(low_key, (TERMS, SECTORS, K), 0, TABLE // 4)
    high = jax.random.randint(high_key, (TERMS, SECTORS, K), 0, TABLE)
    slot = jnp.arange(K, dtype=jnp.int32)[None, None, :]
    values = jnp.where(slot == 0, low, high)
    chosen = jax.random.randint(term_key, (), 0, TERMS)
    term_ids = jnp.arange(TERMS, dtype=jnp.int32)[:, None, None]
    sector_ids = jnp.arange(SECTORS, dtype=jnp.int32)[None, :, None]
    here = (term_ids == chosen) & (sector_ids == 0)
    values = jnp.where(here & (slot == 1), TABLE - 1, values)
    values = jnp.where(here & (slot == 0), 0, values)
    return values.astype(jnp.int32)


def draw_sixj_table(key, part):
    wide_key, near_key = jax.random.split(jax.random.fold_in(key, 23))
    wide = jax.random.uniform(wide_key, (TABLE,), jnp.float32, -1.0, 1.0)
    near = jax.random.uniform(near_key, (TABLE,), jnp.float32, 0.6, 1.0)
    return jnp.where(jnp.arange(TABLE) < TABLE // 4, near, wide).astype(jnp.float32)


def block_levels(stream_key, dims, cuts, smallest, largest):
    def one(axis_at, shards_of):
        draws = jax.random.uniform(jax.random.fold_in(jax.random.fold_in(stream_key, 6), axis_at), (shards_of,), jnp.float32, smallest / len(cuts), largest / len(cuts))
        return jnp.repeat(jnp.exp(draws), dims[axis_at] // shards_of).reshape((-1,) + (1,) * (len(dims) - axis_at - 1))

    gain = one(*cuts[0])
    for cut in cuts[1:]:
        gain = gain * one(*cut)
    return gain


def normal_values(own_key, shape, scale, most, shards=(), kind=jnp.bfloat16):
    drawn = jax.random.normal(own_key, shape, jnp.float32) * scale
    if len(shards) > 0:
        drawn = block_levels(own_key, shape, shards, -0.22, 0.18) * drawn
    return jnp.clip(drawn, min=-most, max=most).astype(kind)


def setup_inputs(seed: int = 0) -> dict:
    seeds = jax.random.split(jax.random.key(seed), 8)
    return {
        "two_site": normal_values(seeds[0], (SEGS, SECTORS, M, M), 1.0, 6.0, ((0, 8), (1, 16)), jnp.float32),
        "left_env": draw_left_env(jax.random.fold_in(seeds[7], 71), 0),
        "right_env": draw_right_env(jax.random.fold_in(seeds[7], 71), 0),
        "block_dims": draw_block_dims(jax.random.fold_in(seeds[7], 71), 0),
        "sources": draw_sources(jax.random.fold_in(seeds[7], 71), 0),
        "sixj_index": draw_sixj_index(jax.random.fold_in(seeds[7], 71), 0),
        "sixj_table": draw_sixj_table(jax.random.fold_in(seeds[7], 71), 0),
    }


step_size = 0.1
epsilon = 1e-06

def coefficients(sources, sixj_index, sixj_table, sector_count):
    levels = jnp.arange(sixj_table.shape[0], dtype=jnp.int32)
    picked = lax.optimization_barrier(jnp.sum(jnp.where(sixj_index[..., None] == levels, sixj_table, jnp.zeros_like(sixj_table)), axis=-1))
    sectors = jnp.arange(sector_count, dtype=jnp.int32)
    spread = jnp.where(sources[..., None] == sectors, picked[..., None], jnp.zeros_like(picked[..., None]))
    return lax.optimization_barrier(jnp.sum(spread, axis=2)).astype(jnp.bfloat16)

def block_mask(block_dims, width):
    rows = (jnp.arange(width, dtype=jnp.int32)[None, :] < block_dims[:, None]).astype(jnp.float32)
    return rows[:, :, None] * rows[:, None, :]

def apply_terms(rounded, coupling, left_blocks, right_blocks, mask):
    mixed = jnp.einsum('wba,aij->wbij', coupling.astype(jnp.float32), rounded.astype(jnp.float32)).astype(jnp.bfloat16)
    right_part = jnp.einsum('wbij,wbjk->wbik', mixed.astype(jnp.float32), right_blocks.astype(jnp.float32)).astype(jnp.bfloat16)
    image = jnp.einsum('wbij,wbjk->bik', left_blocks.astype(jnp.float32), right_part.astype(jnp.float32))
    return image * mask

def segment(two_site, left_blocks, right_blocks, coupling, mask):
    volume = float(SECTORS * M * M)
    state = two_site * mask
    state = state * lax.rsqrt(jnp.sum(state * state) / volume + epsilon)
    for iteration in range(ITERS):
        rounded = state.astype(jnp.bfloat16)
        image = apply_terms(rounded, coupling, left_blocks, right_blocks, mask)
        rayleigh = jnp.sum(state * image) / jnp.sum(state * state)
        state = state - step_size * (image - rayleigh * state)
        state = state * lax.rsqrt(jnp.sum(state * state) / volume + epsilon)
    rounded = state.astype(jnp.bfloat16)
    image = apply_terms(rounded, coupling, left_blocks, right_blocks, mask)
    energy = jnp.sum(state * image) / jnp.sum(state * state)
    inner = jnp.einsum('wbij,bjk->wbik', left_blocks.astype(jnp.float32), rounded.astype(jnp.float32)).astype(jnp.bfloat16)
    fresh = jnp.einsum('bji,wbjk->wbik', rounded.astype(jnp.float32), inner.astype(jnp.float32)) / math.sqrt(M)
    return (rounded, energy, fresh.astype(jnp.bfloat16))

def reference(two_site, left_env, right_env, block_dims, sources, sixj_index, sixj_table):
    coupling = coefficients(sources, sixj_index, sixj_table, SECTORS)
    mask = block_mask(block_dims, M)

    def one_segment(segment_items):
        return segment(segment_items[0], segment_items[1], segment_items[2], coupling, mask)
    solution, energy, fresh = lax.map(one_segment, (two_site, left_env, right_env))
    handoff = jnp.concatenate([left_env[:1], fresh[:-1]], axis=0)
    return (solution, energy, handoff)
```

```python
import jax
import jax.numpy as jnp
from jax import lax
from jax.experimental import pallas as pl
from jax.experimental.pallas import tpu as pltpu
from jax.sharding import PartitionSpec as P

ITERS = 4
STEP = 0.1
EPSILON = 1e-06
MESH = pl.DeviceIdType.MESH
F32 = jnp.float32
BF16 = jnp.bfloat16


def place(distance, ring):
    half = ring // 2
    return jnp.where(
        distance == 0,
        0,
        jnp.where(
            distance < half,
            2 * distance - 1,
            jnp.where(distance == half, ring - 1, 2 * (ring - distance)),
        ),
    )


def place_static(distance, ring):
    half = ring // 2
    if distance == 0:
        return 0
    if distance < half:
        return 2 * distance - 1
    return ring - 1 if distance == half else 2 * (ring - distance)


def build(segments, sectors, terms_axis, terms, couplings, width):
    ring = sectors // 2
    quarter = width // terms_axis
    gathers = ITERS + 1
    volume = float(sectors * width * width)
    chunks = [(0, 1)]
    for reach in range(1, ring // 2):
        chunks.append((2 * reach - 1, 2))
    start, size = chunks.pop()
    chunks.append((start, size + 1))
    n_chunks = len(chunks)

    def kernel(
        two_site, left_hbm, right_hbm, dims, sources, sixj_index, sixj_table,
        solution_out, energy_out, handoff_out,
        left, right, previous, g0, g1, g2, g3, g4, mixed, part, outgoing, arrived,
        state_ref, image_ref, next_ref, scalars, scalars_term, block, previous_block,
        load_sem, left_sems, z_sems, x_sems, core_sems, rs_sems, sz_sems, sx_sems, sol_sems, sol_y_sems,
    ):
        gathered = (g0, g1, g2, g3, g4)
        y = lax.axis_index("chain")
        b = lax.axis_index("sector")
        t = lax.axis_index("term")
        z = b // 2
        c = b % 2

        def wrap(value, count):
            return lax.rem(value + count, count)

        def at_term(step):
            return (y, b, wrap(t + step, terms_axis))

        def at_sector(dz, dc):
            return (y, wrap(z + dz, ring) * 2 + wrap(c + dc, 2), t)

        def at_segment(dy, dt):
            return (wrap(y + dy, segments), b, wrap(t + dt, terms_axis))

        term_steps = (1, terms_axis - 1) + tuple(range(2, terms_axis - 1))
        sector_steps = [(dz, dc) for dz in range(ring) for dc in range(2) if (dz, dc) != (0, 0)]
        my_rows = pl.ds(pl.multiple_of(t * quarter, quarter), quarter)

        def rows_of(step):
            owner = wrap(t + step, terms_axis)
            return pl.ds(pl.multiple_of(owner * quarter, quarter), quarter)

        load_left = pltpu.make_async_copy(left_hbm.at[0, :, 0], left, load_sem.at[0])
        load_right = pltpu.make_async_copy(right_hbm.at[0, :, 0], right, load_sem.at[1])
        load_right.start()
        load_left.start()

        barrier = pltpu.get_barrier_semaphore()
        for step in term_steps:
            pl.semaphore_signal(barrier, inc=1, device_id=at_term(step), device_id_type=MESH)
        for dz, dc in sector_steps:
            pl.semaphore_signal(barrier, inc=1, device_id=at_sector(dz, dc), device_id_type=MESH)
        for dt in range(terms_axis):
            pl.semaphore_signal(barrier, inc=1, device_id=at_segment(-1, dt), device_id_type=MESH)

        def remote(source, target, sems, index, device):
            copy = pltpu.make_async_remote_copy(
                src_ref=source,
                dst_ref=target,
                send_sem=sems.at[(0,) + index],
                recv_sem=sems.at[(1,) + index],
                device_id=device,
                device_id_type=MESH,
            )
            copy.start()
            return copy

        limit = dims[0]
        row_ids = lax.broadcasted_iota(jnp.int32, (quarter, width), 0) + t * quarter
        column_ids = lax.broadcasted_iota(jnp.int32, (quarter, width), 1)
        mask = jnp.where((row_ids < limit) & (column_ids < limit), 1.0, 0.0).astype(F32)

        state = two_site[0, 0, my_rows, :] * mask
        state_ref[...] = state
        gathered[0][0, my_rows, :] = state.astype(BF16)

        pl.semaphore_wait(barrier, len(term_steps) + len(sector_steps) + terms_axis)

        def send_scalars(k, rows):
            blank = jnp.zeros((8 - len(rows), 128), F32)
            scalars[k, b] = jnp.concatenate(rows + [blank], axis=0)
            return [
                remote(scalars.at[k, b], scalars.at[k, b], sz_sems, (k % 2, i), at_sector(dz, dc))
                for i, (dz, dc) in enumerate(sector_steps)
            ]

        def pass_scalars(k, copies):
            for copy in copies:
                copy.wait()
            scalars_term[k, t] = jnp.sum(scalars[k], axis=0)
            return [
                remote(scalars_term.at[k, t], scalars_term.at[k, t], sx_sems, (k % 2, i), at_term(step))
                for i, step in enumerate(term_steps)
            ]

        def take_scalars(k, copies):
            for copy in copies:
                copy.wait()
            return jnp.sum(jnp.sum(scalars_term[k], axis=0), axis=1, keepdims=True)

        def fold(value):
            columns = jnp.sum(value, axis=0, keepdims=True)
            total = columns[:, 0:128]
            for first in range(128, width, 128):
                total = total + columns[:, first : first + 128]
            return total

        def gather(k, scalar_rows):
            whole = gathered[k]
            parity = k % 2
            z_copies = {}
            for distance in sorted(range(1, ring), key=lambda d: place_static(d, ring)):
                z_copies[distance] = remote(
                    whole.at[0, my_rows],
                    whole.at[place_static(ring - distance, ring), my_rows],
                    z_sems, (parity, distance - 1), at_sector(distance, 0),
                )
            x_copies, core_copies = {}, []

            def spread(index):
                first, count = chunks[index]
                for i, step in enumerate(term_steps):
                    piece = whole.at[pl.ds(first, count), my_rows]
                    x_copies[index, i] = remote(piece, piece, x_sems, (parity, i, index), at_term(step))
                core_copies.append(
                    remote(
                        whole.at[pl.ds(first, count), my_rows],
                        whole.at[pl.ds(ring + first, count), my_rows],
                        core_sems, (parity, 0, index), at_sector(0, 1),
                    )
                )

            spread(0)
            scalar_copies = send_scalars(k - 1, scalar_rows) if k else None
            for index in range(1, n_chunks):
                first, count = chunks[index]
                for distance in range(1, ring):
                    if first <= place_static(ring - distance, ring) < first + count:
                        z_copies[distance].wait_recv()
                spread(index)
            if k:
                scalar_copies = pass_scalars(k - 1, scalar_copies)
            for index in range(n_chunks):
                first, count = chunks[index]
                for i, step in enumerate(term_steps):
                    x_copies[index, i].wait_recv()
                    rows = rows_of(-step)
                    core_copies.append(
                        remote(
                            whole.at[pl.ds(first, count), rows],
                            whole.at[pl.ds(ring + first, count), rows],
                            core_sems, (parity, 1 + i, index), at_sector(0, 1),
                        )
                    )
            totals = take_scalars(k - 1, scalar_copies) if k else None
            for copy in core_copies:
                copy.wait_recv()
            sent = list(z_copies.values()) + list(x_copies.values()) + core_copies
            return totals, sent

        def sector_place(sector):
            return wrap(sector % 2 + c, 2) * ring + place(wrap(sector // 2 - z + ring, ring), ring)

        def apply_terms(whole):
            part[...] = jnp.zeros_like(part)

            def one(w, _):
                spots = [sector_place(sources[w, 0, i]) for i in range(couplings)]
                weights = [sixj_table[sixj_index[w, 0, i]] for i in range(couplings)]
                for first in range(0, width, 64):
                    rows = pl.ds(first, 64)
                    total = weights[0] * whole[spots[0], rows, :].astype(F32)
                    for i in range(1, couplings):
                        total = total + weights[i] * whole[spots[i], rows, :].astype(F32)
                    mixed[rows, :] = total.astype(BF16)
                right_part = jnp.dot(mixed[...], right[w], preferred_element_type=F32).astype(BF16)
                part[...] += jnp.dot(left[w], right_part, preferred_element_type=F32)
                return 0

            lax.fori_loop(0, terms, one, 0)

        def reduce_image(k):
            outgoing[...] = part[...].astype(BF16)
            copies = [
                remote(outgoing.at[rows_of(step)], arrived.at[k, i], rs_sems, (k % 2, i), at_term(step))
                for i, step in enumerate(term_steps)
            ]
            total = part[my_rows, :]
            for i, copy in enumerate(copies):
                copy.wait()
                total = total + arrived[k, i].astype(F32)
            return total * mask

        def corrected(k, totals, scale, shift):
            norm, cross, square = totals[0:1], totals[1:2], totals[2:3]
            delta = 1.0 - cross / norm
            grown = square + 2.0 * delta * cross + delta * delta * norm
            if k == 0:
                scale = lax.rsqrt(norm / volume + EPSILON)
                sigma = scale * lax.rsqrt(scale * scale * (grown / volume) + EPSILON)
            else:
                sigma = lax.rsqrt(grown / volume + EPSILON)
            return delta, sigma, shift + delta

        load_left.wait()
        left_copy = remote(left, previous, left_sems, (), at_segment(1, 0))
        load_right.wait()

        shift = jnp.zeros((1, 1), F32)
        rows = None
        for k in range(ITERS):
            totals, sent = gather(k, rows)
            if k:
                delta, sigma, shift = corrected(k - 1, totals, None, shift)
                state_ref[...] = sigma * (next_ref[...] + delta * state_ref[...])
            apply_terms(gathered[k])
            image = reduce_image(k)
            if k:
                image = sigma * (image + delta * image_ref[...])
            image_ref[...] = image
            state = state_ref[...]
            following = (1.0 + shift) * state - STEP * image
            next_ref[...] = following
            gathered[k + 1][0, my_rows, :] = following.astype(BF16)
            rows = [fold(state * state), fold(following * state), fold(following * following)]
            for copy in sent:
                copy.wait_send()

        totals, sent = gather(ITERS, rows)
        delta, sigma, shift = corrected(ITERS - 1, totals, None, shift)
        state = sigma * (next_ref[...] + delta * state_ref[...])
        block[my_rows, :] = state.astype(BF16)
        block_copies = [
            remote(block.at[my_rows], block.at[my_rows], sol_sems, (i,), at_term(step))
            for i, step in enumerate(term_steps)
        ]
        onward = [
            remote(block.at[my_rows], previous_block.at[my_rows], sol_y_sems, (dt,), at_segment(1, dt))
            for dt in range(terms_axis)
        ]
        apply_terms(gathered[ITERS])
        for copy in block_copies:
            copy.wait()
        solution_out[0, 0] = block[...]
        overlap = fold(part[...] * block[...].astype(F32)) + fold(delta * state * image_ref[...])
        energy_copies = send_scalars(ITERS, [fold(state * state), sigma * overlap])
        for copy in sent:
            copy.wait_send()

        left_copy.wait()
        for copy in onward:
            copy.wait()
        energy_copies = pass_scalars(ITERS, energy_copies)

        @pl.when(y == 0)
        def _():
            handoff_out[0, :, 0] = left[...]

        @pl.when(y != 0)
        def _():
            mixed[...] = previous_block[...].T

            def one(w, _):
                inner = jnp.dot(previous[w], previous_block[...], preferred_element_type=F32).astype(BF16)
                fresh = jnp.dot(mixed[...], inner, preferred_element_type=F32) * (1.0 / width**0.5)
                handoff_out[0, w, 0] = fresh.astype(BF16)
                return 0

            lax.fori_loop(0, terms, one, 0)

        totals = take_scalars(ITERS, energy_copies)
        energy_out[...] = jnp.broadcast_to(totals[1:2] / totals[0:1], (1, 128))

    square = (width, width)
    vmem = pl.BlockSpec(memory_space=pltpu.VMEM)
    smem = pl.BlockSpec(memory_space=pltpu.SMEM)
    anywhere = pl.BlockSpec(memory_space=pl.ANY)
    others = terms_axis - 1
    dma = pltpu.SemaphoreType.DMA
    return pl.pallas_call(
        kernel,
        out_shape=(
            jax.ShapeDtypeStruct((1, 1) + square, BF16),
            jax.ShapeDtypeStruct((1, 128), F32),
            jax.ShapeDtypeStruct((1, terms, 1) + square, BF16),
        ),
        in_specs=[vmem, anywhere, anywhere, smem, smem, smem, smem],
        out_specs=(vmem, vmem, vmem),
        scratch_shapes=[
            pltpu.VMEM((terms,) + square, BF16),
            pltpu.VMEM((terms,) + square, BF16),
            pltpu.VMEM((terms,) + square, BF16),
        ]
        + [pltpu.VMEM((sectors,) + square, BF16)] * gathers
        + [
            pltpu.VMEM(square, BF16),
            pltpu.VMEM(square, F32),
            pltpu.VMEM(square, BF16),
            pltpu.VMEM((ITERS, others, quarter, width), BF16),
            pltpu.VMEM((quarter, width), F32),
            pltpu.VMEM((quarter, width), F32),
            pltpu.VMEM((quarter, width), F32),
            pltpu.VMEM((gathers, sectors, 8, 128), F32),
            pltpu.VMEM((gathers, terms_axis, 8, 128), F32),
            pltpu.VMEM(square, BF16),
            pltpu.VMEM(square, BF16),
            dma((2,)),
            dma((2,)),
            dma((2, 2, ring - 1)),
            dma((2, 2, others, n_chunks)),
            dma((2, 2, terms_axis, n_chunks)),
            dma((2, 2, others)),
            dma((2, 2, sectors - 1)),
            dma((2, 2, others)),
            dma((2, others)),
            dma((2, terms_axis)),
        ],
        compiler_params=pltpu.CompilerParams(
            collective_id=1, has_side_effects=True, vmem_limit_bytes=48 * 1024 * 1024
        ),
    )


def solution(mesh):
    def local(two_site, left_env, right_env, block_dims, sources, sixj_index, sixj_table):
        call = build(
            mesh.shape["chain"], mesh.shape["sector"], mesh.shape["term"],
            left_env.shape[1], sources.shape[2], two_site.shape[2],
        )
        state, energy, handoff = call(
            two_site, left_env, right_env, block_dims, sources, sixj_index, sixj_table
        )
        return state, energy[0, 0:1], handoff

    return jax.shard_map(
        local,
        mesh=mesh,
        in_specs=(
            P("chain", "sector", None, None),
            P("chain", "term", "sector", None, None),
            P("chain", "term", "sector", None, None),
            P("sector"),
            P("term", "sector", None),
            P("term", "sector", None),
            P(),
        ),
        out_specs=(
            P("chain", "sector", None, None),
            P("chain"),
            P("chain", "term", "sector", None, None),
        ),
        check_vma=False,
    )
```

```python
import jax
import jax.numpy as jnp
from jax import lax
from jax.experimental import pallas as pl
from jax.experimental.pallas import tpu as pltpu
from jax.sharding import PartitionSpec as P

ITERS = 4
STEP = 0.1
EPSILON = 1e-06
MESH = pl.DeviceIdType.MESH
F32 = jnp.float32
BF16 = jnp.bfloat16


def place(distance, ring):
    half = ring // 2
    return jnp.where(
        distance == 0,
        0,
        jnp.where(
            distance < half,
            2 * distance - 1,
            jnp.where(distance == half, ring - 1, 2 * (ring - distance)),
        ),
    )


def place_static(distance, ring):
    half = ring // 2
    if distance == 0:
        return 0
    if distance < half:
        return 2 * distance - 1
    return ring - 1 if distance == half else 2 * (ring - distance)


def build(segments, sectors, terms_axis, terms, couplings, levels, width):
    ring = sectors // 2
    quarter = width // terms_axis
    gathers = ITERS + 1
    volume = float(sectors * width * width)
    chunks = [(0, 1)]
    for reach in range(1, ring // 2):
        chunks.append((2 * reach - 1, 2))
    chunks.append((ring - 1, 1))
    near_first = sorted(range(1, ring), key=lambda d: place_static(d, ring))
    late = 16
    turn_at = 3
    n_chunks = len(chunks)

    def kernel(
        two_site_hbm, left_hbm, right_hbm, dims_hbm, sources_hbm, index_hbm, table_hbm,
        solution_out, energy_out, handoff_out,
        two_site, dims, sources, sixj_index, sixj_table, left, right, previous, g0, g1, g2, g3, g4, mixed, right_part, part, outgoing, arrived,
        state_ref, image_ref, next_ref, scalars, scalars_term, block, previous_block,
        load_sem, left_sems, z_sems, x_sems, core_sems, rs_sems, sz_sems, sx_sems, sol_sems, sol_y_sems,
    ):
        gathered = (g0, g1, g2, g3, g4)
        y = lax.axis_index("chain")
        b = lax.axis_index("sector")
        t = lax.axis_index("term")
        z = b // 2
        c = b % 2

        def wrap(value, count):
            return lax.rem(value + count, count)

        def at_term(step):
            return (y, b, wrap(t + step, terms_axis))

        def at_sector(dz, dc):
            return (y, wrap(z + dz, ring) * 2 + wrap(c + dc, 2), t)

        def at_segment(dy, dt):
            return (wrap(y + dy, segments), b, wrap(t + dt, terms_axis))

        term_steps = (1, terms_axis - 1) + tuple(range(2, terms_axis - 1))
        sector_steps = [(dz, dc) for dz in range(ring) for dc in range(2) if (dz, dc) != (0, 0)]
        my_rows = pl.ds(pl.multiple_of(t * quarter, quarter), quarter)

        def rows_of(step):
            owner = wrap(t + step, terms_axis)
            return pl.ds(pl.multiple_of(owner * quarter, quarter), quarter)

        load_left = pltpu.make_async_copy(left_hbm.at[0, :, 0], left, load_sem.at[0])
        load_right = pltpu.make_async_copy(right_hbm.at[0, :, 0], right, load_sem.at[1])
        small = [
            pltpu.make_async_copy(source, target, load_sem.at[2 + i])
            for i, (source, target) in enumerate([
                (two_site_hbm.at[0, 0], two_site), (dims_hbm, dims), (sources_hbm, sources),
                (index_hbm, sixj_index), (table_hbm, sixj_table),
            ])
        ]
        for copy in small:
            copy.start()
        load_right.start()
        load_left.start()

        barrier = pltpu.get_barrier_semaphore()
        for step in term_steps:
            pl.semaphore_signal(barrier, inc=1, device_id=at_term(step), device_id_type=MESH)
        for dz, dc in sector_steps:
            pl.semaphore_signal(barrier, inc=1, device_id=at_sector(dz, dc), device_id_type=MESH)
        for dt in range(terms_axis):
            pl.semaphore_signal(barrier, inc=1, device_id=at_segment(-1, dt), device_id_type=MESH)

        def remote(source, target, sems, index, device):
            copy = pltpu.make_async_remote_copy(
                src_ref=source,
                dst_ref=target,
                send_sem=sems.at[(0,) + index],
                recv_sem=sems.at[(1,) + index],
                device_id=device,
                device_id_type=MESH,
            )
            copy.start()
            return copy

        for copy in small:
            copy.wait()
        limit = dims[0]
        row_ids = lax.broadcasted_iota(jnp.int32, (quarter, width), 0) + t * quarter
        column_ids = lax.broadcasted_iota(jnp.int32, (quarter, width), 1)
        mask = jnp.where((row_ids < limit) & (column_ids < limit), 1.0, 0.0).astype(F32)

        state = two_site[my_rows, :] * mask
        state_ref[...] = state
        gathered[0][0, t] = state.astype(BF16)

        pl.semaphore_wait(barrier, len(term_steps) + len(sector_steps) + terms_axis)

        lanes = lax.broadcasted_iota(jnp.int32, (1, 128), 1)

        def fold(value):
            return jnp.sum(jnp.sum(value, axis=0, keepdims=True), axis=1, keepdims=True)

        def send_scalars(k, values):
            packed = jnp.zeros((1, 128), F32)
            for i, value in enumerate(values):
                packed = jnp.where(lanes == i, value, packed)
            scalars[k, b] = packed
            return [
                remote(scalars.at[k, b], scalars.at[k, b], sz_sems, (k % 2, i), at_sector(dz, dc))
                for i, (dz, dc) in enumerate(sector_steps)
            ]

        def pass_scalars(k, copies):
            for copy in copies:
                copy.wait()
            scalars_term[k, t] = jnp.sum(scalars[k], axis=0)
            return [
                remote(scalars_term.at[k, t], scalars_term.at[k, t], sx_sems, (k % 2, i), at_term(step))
                for i, step in enumerate(term_steps)
            ]

        def take_scalars(k, copies, count):
            for copy in copies:
                copy.wait()
            total = jnp.sum(scalars_term[k], axis=0)
            return [
                jnp.sum(jnp.where(lanes == i, total, 0.0), axis=1, keepdims=True) for i in range(count)
            ]

        def gather(k, values, use_totals):
            whole = gathered[k]
            parity = k % 2
            x_copies, z_copies, late_copies, core_copies = {}, {}, {}, []
            everything = pl.ds(0, quarter)

            def early_rows(hops):
                return {1: 0, 2: quarter - late}.get(hops, quarter)

            def hops_of(distance):
                return min(distance, ring - distance)

            def members(index):
                first, count = chunks[index]
                return [
                    d for d in range(1, ring) if first <= place_static(ring - d, ring) < first + count
                ]

            def to_terms(index, rows):
                first, count = chunks[index]
                piece = whole.at[pl.ds(first, count), t, rows]
                for i, step in enumerate(term_steps):
                    x_copies[index, i] = remote(piece, piece, x_sems, (parity, i, index), at_term(step))

            def to_core(index):
                first, count = chunks[index]
                core_copies.append(
                    remote(
                        whole.at[pl.ds(first, count)], whole.at[pl.ds(ring + first, count)],
                        core_sems, (parity, index), at_sector(0, 1),
                    )
                )

            to_terms(0, everything)
            for distance in near_first:
                count = early_rows(hops_of(distance))
                if count:
                    z_copies[distance] = remote(
                        whole.at[0, t, pl.ds(0, count)],
                        whole.at[place_static(ring - distance, ring), t, pl.ds(0, count)],
                        z_sems, (parity, 0, distance - 1), at_sector(distance, 0),
                    )
            scalar_copies = send_scalars(k - 1, values) if k else None

            def turn():
                for i in range(len(term_steps)):
                    x_copies[0, i].wait_recv()
                for distance in near_first:
                    count = early_rows(hops_of(distance))
                    if count < quarter:
                        rows = pl.ds(count, quarter - count)
                        late_copies[distance] = remote(
                            whole.at[0, :, rows],
                            whole.at[place_static(ring - distance, ring), :, rows],
                            z_sems, (parity, 1, distance - 1), at_sector(distance, 0),
                        )
                to_core(0)

            for index in range(2, n_chunks):
                if index == turn_at:
                    turn()
                for distance in members(index):
                    z_copies[distance].wait_recv()
                to_terms(index, pl.ds(0, early_rows(hops_of(members(index)[0]))))
            if k:
                scalar_copies = pass_scalars(k - 1, scalar_copies)
            for index in range(1, n_chunks):
                for distance in members(index):
                    if distance in late_copies:
                        late_copies[distance].wait_recv()
                if index > 1:
                    for i in range(len(term_steps)):
                        x_copies[index, i].wait_recv()
                to_core(index)
                if k and index == n_chunks - 2:
                    use_totals(take_scalars(k - 1, scalar_copies, 3))
            for copy in core_copies:
                copy.wait_recv()
            sent = list(z_copies.values()) + list(late_copies.values()) + list(x_copies.values())
            return sent + core_copies

        def sector_place(sector):
            return wrap(sector % 2 + c, 2) * ring + place(wrap(sector // 2 - z + ring, ring), ring)

        def apply_terms(whole):
            for w in range(terms):
                spots = [sector_place(sources[i, 0, w]) for i in range(couplings)]
                weights = [sixj_table[sixj_index[i, 0, w]] for i in range(couplings)]
                for q in range(terms_axis):
                    total = weights[0] * whole[spots[0], q].astype(F32)
                    for i in range(1, couplings):
                        total = total + weights[i] * whole[spots[i], q].astype(F32)
                    mixed[w, pl.ds(q * quarter, quarter), :] = total.astype(BF16)
                right_part[w] = jnp.dot(mixed[w], right[w], preferred_element_type=F32).astype(BF16)
            total = None
            for w in range(terms):
                product = jnp.dot(left[w], right_part[w], preferred_element_type=F32)
                total = product if total is None else total + product
            part[...] = total

        def reduce_image(k):
            outgoing[...] = part[...].astype(BF16)
            copies = [
                remote(outgoing.at[rows_of(step)], arrived.at[k, i], rs_sems, (k % 2, i), at_term(step))
                for i, step in enumerate(term_steps)
            ]
            total = part[my_rows, :]
            for i, copy in enumerate(copies):
                copy.wait()
                total = total + arrived[k, i].astype(F32)
            return total * mask

        def corrected(k, totals, shift):
            norm, cross, square = totals
            delta = 1.0 - cross / norm
            grown = square + 2.0 * delta * cross + delta * delta * norm
            if k == 0:
                scale = lax.rsqrt(norm / volume + EPSILON)
                sigma = scale * lax.rsqrt(scale * scale * (grown / volume) + EPSILON)
            else:
                sigma = lax.rsqrt(grown / volume + EPSILON)
            state = sigma * (next_ref[...] + delta * state_ref[...])
            state_ref[...] = state
            return delta, sigma, shift + delta, state

        load_left.wait()
        left_copy = remote(left, previous, left_sems, (), at_segment(1, 0))
        load_right.wait()

        known = {"shift": jnp.zeros((1, 1), F32)}

        def step_totals(k):
            def use(totals):
                known["delta"], known["sigma"], known["shift"], _ = corrected(k, totals, known["shift"])

            return use

        values = None
        for k in range(ITERS):
            sent = gather(k, values, step_totals(k - 1))
            apply_terms(gathered[k])
            image = reduce_image(k)
            if k:
                image = known["sigma"] * (image + known["delta"] * image_ref[...])
            image_ref[...] = image
            state = state_ref[...]
            following = (1.0 + known["shift"]) * state - STEP * image
            next_ref[...] = following
            gathered[k + 1][0, t] = following.astype(BF16)
            values = [fold(state * state), fold(following * state), fold(following * following)]
            for copy in sent:
                copy.wait_send()

        block_copies, onward = [], []

        def last_totals(totals):
            known["delta"], known["sigma"], _, state = corrected(ITERS - 1, totals, known["shift"])
            block[my_rows, :] = state.astype(BF16)
            for i, step in enumerate(term_steps):
                block_copies.append(
                    remote(block.at[my_rows], block.at[my_rows], sol_sems, (i,), at_term(step))
                )
            for dt in range(terms_axis):
                onward.append(
                    remote(
                        block.at[my_rows], previous_block.at[my_rows],
                        sol_y_sems, (dt,), at_segment(1, dt),
                    )
                )

        sent = gather(ITERS, values, last_totals)
        apply_terms(gathered[ITERS])
        for copy in block_copies:
            copy.wait()
        solution_out[0, 0] = block[...]
        state = state_ref[...]
        overlap = fold(part[...] * block[...].astype(F32))
        overlap = known["sigma"] * (overlap + known["delta"] * fold(state * image_ref[...]))
        energy_copies = send_scalars(ITERS, [fold(state * state), overlap])
        for copy in sent:
            copy.wait_send()

        left_copy.wait()
        for copy in onward:
            copy.wait()

        @pl.when(y == 0)
        def _():
            handoff_out[0, :, 0] = left[...]

        @pl.when(y != 0)
        def _():
            turned = mixed.at[0]
            turned[...] = previous_block[...].T
            for w in range(terms):
                inner = jnp.dot(previous[w], previous_block[...], preferred_element_type=F32)
                right_part[w] = inner.astype(BF16)
            for w in range(terms):
                fresh = jnp.dot(turned[...], right_part[w], preferred_element_type=F32)
                handoff_out[0, w, 0] = (fresh * (1.0 / width**0.5)).astype(BF16)

        energy_copies = pass_scalars(ITERS, energy_copies)
        norm, overlap = take_scalars(ITERS, energy_copies, 2)
        energy_out[...] = jnp.broadcast_to(overlap / norm, (1, 128))

    square = (width, width)
    vmem = pl.BlockSpec(memory_space=pltpu.VMEM)
    smem = pltpu.SMEM
    held = pl.BlockSpec(memory_space=pl.ANY)
    others = terms_axis - 1
    dma = pltpu.SemaphoreType.DMA
    return pl.pallas_call(
        kernel,
        out_shape=(
            jax.ShapeDtypeStruct((1, 1) + square, BF16),
            jax.ShapeDtypeStruct((1, 128), F32),
            jax.ShapeDtypeStruct((1, terms, 1) + square, BF16),
        ),
        in_specs=[held] * 7,
        out_specs=(vmem, vmem, vmem),
        scratch_shapes=[
            pltpu.VMEM(square, F32),
            smem((1,), jnp.int32),
            smem((couplings, 1, terms), jnp.int32),
            smem((couplings, 1, terms), jnp.int32),
            smem((levels,), F32),
            pltpu.VMEM((terms,) + square, BF16),
            pltpu.VMEM((terms,) + square, BF16),
            pltpu.VMEM((terms,) + square, BF16),
        ]
        + [pltpu.VMEM((sectors, terms_axis, quarter, width), BF16)] * gathers
        + [
            pltpu.VMEM((terms,) + square, BF16),
            pltpu.VMEM((terms,) + square, BF16),
            pltpu.VMEM(square, F32),
            pltpu.VMEM(square, BF16),
            pltpu.VMEM((ITERS, others, quarter, width), BF16),
            pltpu.VMEM((quarter, width), F32),
            pltpu.VMEM((quarter, width), F32),
            pltpu.VMEM((quarter, width), F32),
            pltpu.VMEM((gathers, sectors, 1, 128), F32),
            pltpu.VMEM((gathers, terms_axis, 1, 128), F32),
            pltpu.VMEM(square, BF16),
            pltpu.VMEM(square, BF16),
            dma((7,)),
            dma((2,)),
            dma((2, 2, 2, ring - 1)),
            dma((2, 2, others, n_chunks)),
            dma((2, 2, n_chunks)),
            dma((2, 2, others)),
            dma((2, 2, sectors - 1)),
            dma((2, 2, others)),
            dma((2, others)),
            dma((2, terms_axis)),
        ],
        compiler_params=pltpu.CompilerParams(
            collective_id=1, has_side_effects=True, vmem_limit_bytes=56500 * 1024
        ),
    )


def hand_over(state, energy, handoff):
    terms = handoff.shape[1]

    def kernel(state_in, energy_in, handoff_in, state_out, energy_out, handoff_out, a, b, c, sems):
        moves = [(state_in, a, state_out), (energy_in, b, energy_out)] + [
            (handoff_in.at[0, w], c.at[0, w], handoff_out.at[0, w]) for w in range(terms)
        ]
        loads = [pltpu.make_async_copy(m[0], m[1], sems.at[0, i]) for i, m in enumerate(moves)]
        stores = [pltpu.make_async_copy(m[1], m[2], sems.at[1, i]) for i, m in enumerate(moves)]
        for copy in loads:
            copy.start()
        for load, store in zip(loads, stores):
            load.wait()
            store.start()
        for copy in stores:
            copy.wait()

    held = pl.BlockSpec(memory_space=pl.ANY)
    arrays = (state, energy, handoff)
    return pl.pallas_call(
        kernel,
        out_shape=tuple(jax.ShapeDtypeStruct(array.shape, array.dtype) for array in arrays),
        in_specs=[held] * 3,
        out_specs=(held,) * 3,
        scratch_shapes=[pltpu.VMEM(array.shape, array.dtype) for array in arrays]
        + [pltpu.SemaphoreType.DMA((2, terms + 2))],
        compiler_params=pltpu.CompilerParams(vmem_limit_bytes=56500 * 1024),
    )(*arrays)


def solution(mesh):
    def local(two_site, left_env, right_env, block_dims, sources, sixj_index, sixj_table):
        call = build(
            mesh.shape["chain"], mesh.shape["sector"], mesh.shape["term"],
            left_env.shape[1], sources.shape[2], sixj_table.shape[0], two_site.shape[2],
        )
        state, energy, handoff = call(
            two_site, left_env, right_env, block_dims, sources.transpose(2, 1, 0),
            sixj_index.transpose(2, 1, 0), sixj_table
        )
        state, energy, handoff = hand_over(state, energy, handoff)
        return state, energy[0, 0:1], handoff

    return jax.shard_map(
        local,
        mesh=mesh,
        in_specs=(
            P("chain", "sector", None, None),
            P("chain", "term", "sector", None, None),
            P("chain", "term", "sector", None, None),
            P("sector"),
            P("term", "sector", None),
            P("term", "sector", None),
            P(),
        ),
        out_specs=(
            P("chain", "sector", None, None),
            P("chain"),
            P("chain", "term", "sector", None, None),
        ),
        check_vma=False,
    )
```

```python
import jax
import jax.numpy as jnp
from jax import lax
from jax.experimental import pallas as pl
from jax.experimental.pallas import tpu as pltpu
from jax.sharding import PartitionSpec as P

ITERS = 4
STEP = 0.1
EPSILON = 1e-06
MESH = pl.DeviceIdType.MESH
F32 = jnp.float32
BF16 = jnp.bfloat16


def place(distance, ring):
    half = ring // 2
    return jnp.where(
        distance == 0,
        0,
        jnp.where(
            distance < half,
            2 * distance - 1,
            jnp.where(distance == half, ring - 1, 2 * (ring - distance)),
        ),
    )


def place_static(distance, ring):
    half = ring // 2
    if distance == 0:
        return 0
    if distance < half:
        return 2 * distance - 1
    return ring - 1 if distance == half else 2 * (ring - distance)


def build(segments, sectors, terms_axis, terms, couplings, levels, width):
    ring = sectors // 2
    half = width // 2
    strip = half // terms_axis
    quarter = 2 * strip
    gathers = ITERS + 1
    volume = float(sectors * width * width)
    chunks = [(0, 1)]
    for reach in range(1, ring // 2):
        chunks.append((2 * reach - 1, 2))
    chunks.append((ring - 1, 1))
    near_first = sorted(range(1, ring), key=lambda d: place_static(d, ring))
    late = 16
    turn_at = 2
    n_chunks = len(chunks)

    def kernel(
        two_site_hbm, left_hbm, right_hbm, dims_hbm, sources_hbm, index_hbm, table_hbm,
        solution_out, energy_out, handoff_out,
        two_site, dims, sources, sixj_index, sixj_table, left_whole, left, right, previous, g0, g1, g2, g3, g4,
        other_half, mixed, right_part, part, outgoing, arrived, turned,
        state_ref, image_ref, next_ref, scalars, scalars_term, block, previous_block,
        load_sem, left_sems, pair_sems, z_sems, late_sems, own_sems, x_sems, rs_sems, sz_sems, sx_sems, sol_sems, sol_y_sems,
    ):
        gathered = (g0, g1, g2, g3, g4)
        y = lax.axis_index("chain")
        b = lax.axis_index("sector")
        t = lax.axis_index("term")
        z = b // 2
        c = b % 2

        def wrap(value, count):
            return lax.rem(value + count, count)

        def at_term(step):
            return (y, b, wrap(t + step, terms_axis))

        def at_sector(dz, dc):
            return (y, wrap(z + dz, ring) * 2 + wrap(c + dc, 2), t)

        def at_segment(dy, dt):
            return (wrap(y + dy, segments), b, wrap(t + dt, terms_axis))

        term_steps = (1, terms_axis - 1) + tuple(range(2, terms_axis - 1))
        sector_steps = [(dz, dc) for dz in range(ring) for dc in range(2) if (dz, dc) != (0, 0)]
        chip_steps = [
            (dt, dc) for dc in range(2) for dt in (0,) + term_steps if (dt, dc) != (0, 0)
        ]

        def at_chip(dt, dc):
            return (y, z * 2 + wrap(c + dc, 2), wrap(t + dt, terms_axis))

        def my_strips(ref):
            low = ref[pl.ds(pl.multiple_of(t * strip, strip), strip), :]
            high = ref[pl.ds(pl.multiple_of(half + t * strip, strip), strip), :]
            return jnp.concatenate([low, high], axis=0)

        def left_half(core):
            return left_hbm.at[0, :, 0, :, pl.ds(pl.multiple_of(core * half, half), half)]

        load_whole = pltpu.make_async_copy(left_hbm.at[0, :, 0], left_whole, load_sem.at[7])
        load_left = pltpu.make_async_copy(left_half(c), left.at[c], load_sem.at[0])
        load_right = pltpu.make_async_copy(right_hbm.at[0, :, 0], right.at[c], load_sem.at[1])
        small = [
            pltpu.make_async_copy(source, target, load_sem.at[2 + i])
            for i, (source, target) in enumerate([
                (two_site_hbm.at[0, 0], two_site), (dims_hbm, dims), (sources_hbm, sources.at[c]),
                (index_hbm, sixj_index.at[c]), (table_hbm, sixj_table),
            ])
        ]
        for copy in small:
            copy.start()
        load_right.start()
        load_whole.start()
        load_left.start()

        barrier = pltpu.get_barrier_semaphore()
        for step in term_steps:
            for dc in range(2):
                pl.semaphore_signal(barrier, inc=1, device_id=at_chip(step, dc), device_id_type=MESH)
        for dz, dc in sector_steps:
            pl.semaphore_signal(barrier, inc=1, device_id=at_sector(dz, dc), device_id_type=MESH)
        for dt in range(terms_axis):
            pl.semaphore_signal(barrier, inc=1, device_id=at_segment(-1, dt), device_id_type=MESH)

        def remote(source, target, sems, index, device):
            copy = pltpu.make_async_remote_copy(
                src_ref=source,
                dst_ref=target,
                send_sem=sems.at[(0,) + index],
                recv_sem=sems.at[(1,) + index],
                device_id=device,
                device_id_type=MESH,
            )
            copy.start()
            return copy

        for copy in small:
            copy.wait()
        limit = dims[0]
        row_ids = lax.broadcasted_iota(jnp.int32, (quarter, width), 0)
        row_ids = t * strip + jnp.where(row_ids < strip, row_ids, row_ids - strip + half)
        column_ids = lax.broadcasted_iota(jnp.int32, (quarter, width), 1)
        mask = jnp.where((row_ids < limit) & (column_ids < limit), 1.0, 0.0).astype(F32)

        def stage(k, value):
            low, high = value[0:strip], value[strip:quarter]
            gathered[k][c, t] = jnp.where(c == 0, low, high).astype(BF16)
            other_half[k] = jnp.where(c == 0, high, low).astype(BF16)

        state = my_strips(two_site) * mask
        state_ref[...] = state
        stage(0, state)

        pl.semaphore_wait(barrier, 2 * len(term_steps) + len(sector_steps) + terms_axis)

        lanes = lax.broadcasted_iota(jnp.int32, (1, 128), 1)

        def fold(value):
            return jnp.sum(jnp.sum(value, axis=0, keepdims=True), axis=1, keepdims=True)

        def send_scalars(k, values):
            packed = jnp.zeros((1, 128), F32)
            for i, value in enumerate(values):
                packed = jnp.where(lanes == i, value, packed)
            scalars[k, b] = packed
            return [
                remote(scalars.at[k, b], scalars.at[k, b], sz_sems, (k % 2, i), at_sector(dz, dc))
                for i, (dz, dc) in enumerate(sector_steps)
            ]

        def pass_scalars(k, copies):
            for copy in copies:
                copy.wait()
            scalars_term[k, t] = jnp.sum(scalars[k], axis=0)
            return [
                remote(scalars_term.at[k, t], scalars_term.at[k, t], sx_sems, (k % 2, i), at_term(step))
                for i, step in enumerate(term_steps)
            ]

        def take_scalars(k, copies, count):
            for copy in copies:
                copy.wait()
            total = jnp.sum(scalars_term[k], axis=0)
            return [
                jnp.sum(jnp.where(lanes == i, total, 0.0), axis=1, keepdims=True) for i in range(count)
            ]

        def gather(k, values, use_totals, before):
            whole = gathered[k]
            other = other_half.at[k]
            parity = k % 2
            x_copies, z_copies, late_copies = {}, {}, {}

            def early_rows(hops):
                return {1: 0, 2: strip - late}.get(hops, strip)

            def hops_of(distance):
                return min(distance, ring - distance)

            def members(index):
                first, count = chunks[index]
                return [
                    d for d in range(1, ring) if first <= place_static(ring - d, ring) < first + count
                ]

            own_copies = [remote(other, whole.at[c, t], own_sems, (parity, 0, 0), at_sector(0, 1))]
            for i, step in enumerate(term_steps):
                own_copies.append(
                    remote(
                        whole.at[c, t], whole.at[c, t], own_sems, (parity, 0, 1 + i), at_chip(step, 0)
                    )
                )
                own_copies.append(
                    remote(other, whole.at[c, t], own_sems, (parity, 1, 1 + i), at_chip(step, 1))
                )
            for distance in near_first:
                count = early_rows(hops_of(distance))
                if count:
                    rows = pl.ds(0, count)
                    target = whole.at[2 * place_static(ring - distance, ring) + c, t, rows]
                    z_copies[distance] = [
                        remote(
                            whole.at[c, t, rows], target,
                            z_sems, (parity, 0, distance - 1), at_sector(distance, 0),
                        ),
                        remote(
                            other.at[rows], target,
                            z_sems, (parity, 1, distance - 1), at_sector(distance, 1),
                        ),
                    ]
            scalar_copies = send_scalars(k - 1, values()) if k else send_environments()

            def turn():
                for copy in own_copies:
                    copy.wait_recv()
                for distance in near_first:
                    count = early_rows(hops_of(distance))
                    if count < strip:
                        rows = pl.ds(count, strip - count)
                        late_copies[distance] = remote(
                            whole.at[pl.ds(0, 2), :, rows],
                            whole.at[pl.ds(2 * place_static(ring - distance, ring), 2), :, rows],
                            late_sems, (parity, distance - 1), at_sector(distance, 0),
                        )

            for index in range(2, n_chunks):
                if index == turn_at:
                    turn()
                for distance in members(index):
                    for copy in z_copies[distance]:
                        copy.wait_recv()
                first, count = chunks[index]
                rows = pl.ds(0, early_rows(hops_of(members(index)[0])))
                piece = whole.at[pl.ds(2 * first, 2 * count), t, rows]
                for i, step in enumerate(term_steps):
                    x_copies[index, i] = remote(piece, piece, x_sems, (parity, i, index), at_term(step))
            if k:
                scalar_copies = pass_scalars(k - 1, scalar_copies)
            for copy in before:
                copy.wait_send()
            for index in range(1, n_chunks):
                if k and index == n_chunks - 1:
                    use_totals(take_scalars(k - 1, scalar_copies, 3))
                for distance in members(index):
                    if distance in late_copies:
                        late_copies[distance].wait_recv()
                if index > 1:
                    for i in range(len(term_steps)):
                        x_copies[index, i].wait_recv()
            sent = own_copies + list(late_copies.values()) + list(x_copies.values())
            return sent + [copy for pair in z_copies.values() for copy in pair]

        def sector_place(sector):
            return 2 * place(wrap(sector // 2 - z + ring, ring), ring) + sector % 2

        def apply_terms(whole, send=None):
            for turn_of in range(2):
                s = wrap(c + 1 - turn_of, 2)
                for w in range(terms):
                    spots = [sector_place(sources[s, i, 0, w]) for i in range(couplings)]
                    weights = [sixj_table[sixj_index[s, i, 0, w]] for i in range(couplings)]
                    for q in range(terms_axis):
                        total = weights[0] * whole[spots[0], q].astype(F32)
                        for i in range(1, couplings):
                            total = total + weights[i] * whole[spots[i], q].astype(F32)
                        mixed[turn_of, w, pl.ds(q * strip, strip), :] = total.astype(BF16)
                    product = jnp.dot(mixed[turn_of, w], right[s, w], preferred_element_type=F32)
                    right_part[turn_of, w // 2, pl.ds(w % 2 * half, half), :] = product.astype(BF16)
                total = None
                for p in range(terms // 2):
                    both = jnp.concatenate([left[s, 2 * p], left[s, 2 * p + 1]], axis=1)
                    product = jnp.dot(both, right_part[turn_of, p], preferred_element_type=F32)
                    total = product if total is None else total + product
                part[turn_of] = total
                if send is not None:
                    send(turn_of)

        def image_of(k, whole):
            copies = []

            def send(turn_of):
                outgoing[turn_of] = part[turn_of].astype(BF16).reshape(2, terms_axis, strip, width)
                for i, (dt, dc) in enumerate(chip_steps):
                    if dc == 1 - turn_of:
                        copies.append(
                            remote(
                                outgoing.at[turn_of, :, wrap(t + dt, terms_axis)], arrived.at[k, i],
                                rs_sems, (k % 2, i), at_chip(dt, dc),
                            )
                        )

            apply_terms(whole, send)
            total = my_strips(part.at[1])
            for copy in copies:
                copy.wait()
            for i in range(len(chip_steps)):
                total = total + arrived[k, i].astype(F32).reshape(quarter, width)
            return total * mask

        def corrected(k, totals, shift):
            norm, cross, square = totals
            delta = 1.0 - cross / norm
            grown = square + 2.0 * delta * cross + delta * delta * norm
            if k == 0:
                scale = lax.rsqrt(norm / volume + EPSILON)
                sigma = scale * lax.rsqrt(scale * scale * (grown / volume) + EPSILON)
            else:
                sigma = lax.rsqrt(grown / volume + EPSILON)
            state = sigma * (next_ref[...] + delta * state_ref[...])
            state_ref[...] = state
            return delta, sigma, shift + delta, state

        sibling = at_sector(0, 1)
        other_columns = pl.ds(pl.multiple_of((1 - c) * half, half), half)
        pair_copies = [
            remote(sources_hbm, sources.at[c], pair_sems, (0,), sibling),
            remote(index_hbm, sixj_index.at[c], pair_sems, (1,), sibling),
        ]

        def send_environments():
            load_right.wait()
            pair_copies.append(remote(right.at[c], right.at[c], pair_sems, (2,), sibling))
            load_whole.wait()
            pair_copies.append(
                remote(left_whole.at[:, :, other_columns], left.at[c], pair_sems, (3,), sibling)
            )
            pair_copies.append(remote(left_whole, previous, left_sems, (), at_segment(1, 0)))
            load_left.wait()

        known = {"shift": jnp.zeros((1, 1), F32)}

        def step_totals(k):
            def use(totals):
                known["delta"], known["sigma"], known["shift"], _ = corrected(k, totals, known["shift"])

            return use

        values, sent = None, []
        for k in range(ITERS):
            sent = gather(k, values, step_totals(k - 1), sent)
            if k == 0:
                for copy in pair_copies[0:4]:
                    copy.wait()
            image = image_of(k, gathered[k])
            if k:
                image = known["sigma"] * (image + known["delta"] * image_ref[...])
            image_ref[...] = image
            state = state_ref[...]
            following = (1.0 + known["shift"]) * state - STEP * image
            next_ref[...] = following
            stage(k + 1, following)

            def values(state=state, following=following):
                return [fold(state * state), fold(following * state), fold(following * following)]


        block_copies, onward = [], []

        def last_totals(totals):
            known["delta"], known["sigma"], _, state = corrected(ITERS - 1, totals, known["shift"])
            block[c, :, t] = state.astype(BF16).reshape(2, strip, width)
            mine = block.at[c, :, t]
            for i, (dt, dc) in enumerate(chip_steps):
                block_copies.append(remote(mine, mine, sol_sems, (i,), at_chip(dt, dc)))
            for dt in range(terms_axis):
                onward.append(
                    remote(mine, previous_block.at[:, t], sol_y_sems, (dt,), at_segment(1, dt))
                )

        sent = gather(ITERS, values, last_totals, sent)
        apply_terms(gathered[ITERS])
        for copy in block_copies:
            copy.wait()
        solution_out[0, 0] = block[c].reshape(width, width)
        state = state_ref[...]
        overlap = part[0] * block[1 - c].reshape(width, width).astype(F32)
        overlap = fold(overlap + part[1] * block[c].reshape(width, width).astype(F32))
        overlap = known["sigma"] * (overlap + known["delta"] * fold(state * image_ref[...]))
        energy_copies = send_scalars(ITERS, [fold(state * state), overlap])
        for copy in sent:
            copy.wait_send()

        pair_copies[4].wait()
        for copy in onward:
            copy.wait()

        @pl.when(y == 0)
        def _():
            handoff_out[0, :, 0] = left_whole[...]

        @pl.when(y != 0)
        def _():
            received = previous_block[...].reshape(width, width)
            turned[...] = received.T
            for w in range(terms):
                inner = jnp.dot(previous[w], received, preferred_element_type=F32)
                right_part[w % 2, w // 2] = inner.astype(BF16)
            for w in range(terms):
                fresh = jnp.dot(turned[...], right_part[w % 2, w // 2], preferred_element_type=F32)
                handoff_out[0, w, 0] = (fresh * (1.0 / width**0.5)).astype(BF16)

        energy_copies = pass_scalars(ITERS, energy_copies)
        norm, overlap = take_scalars(ITERS, energy_copies, 2)
        energy_out[...] = jnp.broadcast_to(overlap / norm, (1, 128))

    square = (width, width)
    vmem = pl.BlockSpec(memory_space=pltpu.VMEM)
    smem = pltpu.SMEM
    held = pl.BlockSpec(memory_space=pl.ANY)
    others = terms_axis - 1
    peers = 2 * terms_axis - 1
    dma = pltpu.SemaphoreType.DMA
    return pl.pallas_call(
        kernel,
        out_shape=(
            jax.ShapeDtypeStruct((1, 1) + square, BF16),
            jax.ShapeDtypeStruct((1, 128), F32),
            jax.ShapeDtypeStruct((1, terms, 1) + square, BF16),
        ),
        in_specs=[held] * 7,
        out_specs=(vmem, vmem, vmem),
        scratch_shapes=[
            pltpu.VMEM(square, F32),
            smem((1,), jnp.int32),
            smem((2, couplings, 1, terms), jnp.int32),
            smem((2, couplings, 1, terms), jnp.int32),
            smem((levels,), F32),
            pltpu.VMEM((terms,) + square, BF16),
            pltpu.VMEM((2, terms, width, half), BF16),
            pltpu.VMEM((2, terms) + square, BF16),
            pltpu.VMEM((terms,) + square, BF16),
        ]
        + [pltpu.VMEM((sectors, terms_axis, strip, width), BF16)] * gathers
        + [
            pltpu.VMEM((gathers, strip, width), BF16),
            pltpu.VMEM((2, terms, half, width), BF16),
            pltpu.VMEM((2, terms // 2) + square, BF16),
            pltpu.VMEM((2,) + square, F32),
            pltpu.VMEM((2, 2, terms_axis, strip, width), BF16),
            pltpu.VMEM((ITERS, peers, 2, strip, width), BF16),
            pltpu.VMEM(square, BF16),
            pltpu.VMEM((quarter, width), F32),
            pltpu.VMEM((quarter, width), F32),
            pltpu.VMEM((quarter, width), F32),
            pltpu.VMEM((gathers, sectors, 1, 128), F32),
            pltpu.VMEM((gathers, terms_axis, 1, 128), F32),
            pltpu.VMEM((2, 2, terms_axis, strip, width), BF16),
            pltpu.VMEM((2, terms_axis, strip, width), BF16),
            dma((8,)),
            dma((2,)),
            dma((2, 4)),
            dma((2, 2, 2, ring - 1)),
            dma((2, 2, ring - 1)),
            dma((2, 2, 2, terms_axis)),
            dma((2, 2, others, n_chunks)),
            dma((2, 2, peers)),
            dma((2, 2, sectors - 1)),
            dma((2, 2, others)),
            dma((2, peers)),
            dma((2, terms_axis)),
        ],
        compiler_params=pltpu.CompilerParams(
            collective_id=1, has_side_effects=True, vmem_limit_bytes=56500 * 1024
        ),
    )


def hand_over(state, energy, handoff):
    terms = handoff.shape[1]

    def kernel(state_in, energy_in, handoff_in, state_out, energy_out, handoff_out, a, b, c, sems):
        moves = [(state_in, a, state_out), (energy_in, b, energy_out)] + [
            (handoff_in.at[0, w], c.at[0, w], handoff_out.at[0, w]) for w in range(terms)
        ]
        loads = [pltpu.make_async_copy(m[0], m[1], sems.at[0, i]) for i, m in enumerate(moves)]
        stores = [pltpu.make_async_copy(m[1], m[2], sems.at[1, i]) for i, m in enumerate(moves)]
        for copy in loads:
            copy.start()
        for load, store in zip(loads, stores):
            load.wait()
            store.start()
        for copy in stores:
            copy.wait()

    held = pl.BlockSpec(memory_space=pl.ANY)
    arrays = (state, energy, handoff)
    return pl.pallas_call(
        kernel,
        out_shape=tuple(jax.ShapeDtypeStruct(array.shape, array.dtype) for array in arrays),
        in_specs=[held] * 3,
        out_specs=(held,) * 3,
        scratch_shapes=[pltpu.VMEM(array.shape, array.dtype) for array in arrays]
        + [pltpu.SemaphoreType.DMA((2, terms + 2))],
        compiler_params=pltpu.CompilerParams(vmem_limit_bytes=56500 * 1024),
    )(*arrays)


def solution(mesh):
    def local(two_site, left_env, right_env, block_dims, sources, sixj_index, sixj_table):
        call = build(
            mesh.shape["chain"], mesh.shape["sector"], mesh.shape["term"],
            left_env.shape[1], sources.shape[2], sixj_table.shape[0], two_site.shape[2],
        )
        state, energy, handoff = call(
            two_site, left_env, right_env, block_dims, sources.transpose(2, 1, 0),
            sixj_index.transpose(2, 1, 0), sixj_table
        )
        state, energy, handoff = hand_over(state, energy, handoff)
        return state, energy[0, 0:1], handoff

    return jax.shard_map(
        local,
        mesh=mesh,
        in_specs=(
            P("chain", "sector", None, None),
            P("chain", "term", "sector", None, None),
            P("chain", "term", "sector", None, None),
            P("sector"),
            P("term", "sector", None),
            P("term", "sector", None),
            P(),
        ),
        out_specs=(
            P("chain", "sector", None, None),
            P("chain"),
            P("chain", "term", "sector", None, None),
        ),
        check_vma=False,
    )
```

```python
import jax
import jax.numpy as jnp
from jax import lax
from jax.experimental import pallas as pl
from jax.experimental.pallas import tpu as pltpu
from jax.sharding import PartitionSpec as P

ITERS = 4
STEP = 0.1
EPSILON = 1e-06
MESH = pl.DeviceIdType.MESH
F32 = jnp.float32
BF16 = jnp.bfloat16


def place(distance, ring):
    half = ring // 2
    return jnp.where(
        distance == 0,
        0,
        jnp.where(
            distance < half,
            2 * distance - 1,
            jnp.where(distance == half, ring - 1, 2 * (ring - distance)),
        ),
    )


def place_static(distance, ring):
    half = ring // 2
    if distance == 0:
        return 0
    if distance < half:
        return 2 * distance - 1
    return ring - 1 if distance == half else 2 * (ring - distance)


def build(segments, sectors, terms_axis, terms, couplings, levels, width):
    ring = sectors // 2
    half = width // 2
    strip = half // terms_axis
    quarter = 2 * strip
    gathers = ITERS + 1
    volume = float(sectors * width * width)
    chunks = [(0, 1)]
    for reach in range(1, ring // 2):
        chunks.append((2 * reach - 1, 2))
    chunks.append((ring - 1, 1))
    near_first = sorted(range(1, ring), key=lambda d: place_static(d, ring))
    late = 16
    turn_at = 2
    n_chunks = len(chunks)

    def kernel(
        two_site_hbm, left_hbm, right_hbm, dims_hbm, sources_hbm, index_hbm, table_hbm,
        solution_out, energy_out, handoff_out,
        two_site, dims, sources, sixj_index, sixj_table, left_whole, left, right, previous, g0, g1, g2, g3, g4,
        other_half, mixed, right_part, part, outgoing, arrived, turned, solved,
        state_ref, image_ref, next_ref, scalars, scalars_term, block, previous_block,
        load_sem, left_sems, pair_sems, z_sems, late_sems, own_sems, x_sems, rs_sems, sz_sems, sx_sems, sol_sems, sol_y_sems,
    ):
        gathered = (g0, g1, g2, g3, g4)
        y = lax.axis_index("chain")
        b = lax.axis_index("sector")
        t = lax.axis_index("term")
        z = b // 2
        c = b % 2

        def wrap(value, count):
            return lax.rem(value + count, count)

        def at_term(step):
            return (y, b, wrap(t + step, terms_axis))

        def at_sector(dz, dc):
            return (y, wrap(z + dz, ring) * 2 + wrap(c + dc, 2), t)

        def at_segment(dy, dt):
            return (wrap(y + dy, segments), b, wrap(t + dt, terms_axis))

        term_steps = (1, terms_axis - 1) + tuple(range(2, terms_axis - 1))
        sector_steps = [(dz, dc) for dz in range(ring) for dc in range(2) if (dz, dc) != (0, 0)]
        chip_steps = [
            (dt, dc) for dc in range(2) for dt in (0,) + term_steps if (dt, dc) != (0, 0)
        ]

        def at_chip(dt, dc):
            return (y, z * 2 + wrap(c + dc, 2), wrap(t + dt, terms_axis))

        def my_strips(ref):
            low = ref[pl.ds(pl.multiple_of(t * strip, strip), strip), :]
            high = ref[pl.ds(pl.multiple_of(half + t * strip, strip), strip), :]
            return jnp.concatenate([low, high], axis=0)

        def left_half(core):
            return left_hbm.at[0, :, 0, :, pl.ds(pl.multiple_of(core * half, half), half)]

        load_whole = pltpu.make_async_copy(left_hbm.at[0, :, 0], left_whole, load_sem.at[7])
        load_left = pltpu.make_async_copy(left_half(c), left.at[c], load_sem.at[0])
        load_right = pltpu.make_async_copy(right_hbm.at[0, :, 0], right.at[c], load_sem.at[1])
        small = [
            pltpu.make_async_copy(source, target, load_sem.at[2 + i])
            for i, (source, target) in enumerate([
                (two_site_hbm.at[0, 0], two_site), (dims_hbm, dims), (sources_hbm, sources.at[c]),
                (index_hbm, sixj_index.at[c]), (table_hbm, sixj_table),
            ])
        ]
        for copy in small:
            copy.start()
        load_right.start()
        load_whole.start()
        load_left.start()

        barrier = pltpu.get_barrier_semaphore()
        for step in term_steps:
            for dc in range(2):
                pl.semaphore_signal(barrier, inc=1, device_id=at_chip(step, dc), device_id_type=MESH)
        for dz, dc in sector_steps:
            pl.semaphore_signal(barrier, inc=1, device_id=at_sector(dz, dc), device_id_type=MESH)
        for dt in range(terms_axis):
            pl.semaphore_signal(barrier, inc=1, device_id=at_segment(-1, dt), device_id_type=MESH)

        def remote(source, target, sems, index, device):
            copy = pltpu.make_async_remote_copy(
                src_ref=source,
                dst_ref=target,
                send_sem=sems.at[(0,) + index],
                recv_sem=sems.at[(1,) + index],
                device_id=device,
                device_id_type=MESH,
            )
            copy.start()
            return copy

        for copy in small:
            copy.wait()
        limit = dims[0]
        row_ids = lax.broadcasted_iota(jnp.int32, (quarter, width), 0)
        row_ids = t * strip + jnp.where(row_ids < strip, row_ids, row_ids - strip + half)
        column_ids = lax.broadcasted_iota(jnp.int32, (quarter, width), 1)
        mask = jnp.where((row_ids < limit) & (column_ids < limit), 1.0, 0.0).astype(F32)

        def stage(k, value):
            low, high = value[0:strip], value[strip:quarter]
            gathered[k][c, t] = jnp.where(c == 0, low, high).astype(BF16)
            other_half[k] = jnp.where(c == 0, high, low).astype(BF16)

        state = my_strips(two_site) * mask
        state_ref[...] = state
        stage(0, state)

        pl.semaphore_wait(barrier, 2 * len(term_steps) + len(sector_steps) + terms_axis)

        lanes = lax.broadcasted_iota(jnp.int32, (1, 128), 1)

        def fold(value):
            return jnp.sum(jnp.sum(value, axis=0, keepdims=True), axis=1, keepdims=True)

        def send_scalars(k, values):
            packed = jnp.zeros((1, 128), F32)
            for i, value in enumerate(values):
                packed = jnp.where(lanes == i, value, packed)
            scalars[k, b] = packed
            return [
                remote(scalars.at[k, b], scalars.at[k, b], sz_sems, (k % 2, i), at_sector(dz, dc))
                for i, (dz, dc) in enumerate(sector_steps)
            ]

        def pass_scalars(k, copies):
            for copy in copies:
                copy.wait()
            scalars_term[k, t] = jnp.sum(scalars[k], axis=0)
            return [
                remote(scalars_term.at[k, t], scalars_term.at[k, t], sx_sems, (k % 2, i), at_term(step))
                for i, step in enumerate(term_steps)
            ]

        def take_scalars(k, copies, count):
            for copy in copies:
                copy.wait()
            total = jnp.sum(scalars_term[k], axis=0)
            return [
                jnp.sum(jnp.where(lanes == i, total, 0.0), axis=1, keepdims=True) for i in range(count)
            ]

        def gather(k, values, use_totals, before):
            whole = gathered[k]
            other = other_half.at[k]
            parity = k % 2
            x_copies, z_copies, late_copies = {}, {}, {}

            def early_rows(hops):
                return {1: 0, 2: strip - late}.get(hops, strip)

            def hops_of(distance):
                return min(distance, ring - distance)

            def members(index):
                first, count = chunks[index]
                return [
                    d for d in range(1, ring) if first <= place_static(ring - d, ring) < first + count
                ]

            own_copies = [remote(other, whole.at[c, t], own_sems, (parity, 0, 0), at_sector(0, 1))]
            for i, step in enumerate(term_steps):
                own_copies.append(
                    remote(
                        whole.at[c, t], whole.at[c, t], own_sems, (parity, 0, 1 + i), at_chip(step, 0)
                    )
                )
                own_copies.append(
                    remote(other, whole.at[c, t], own_sems, (parity, 1, 1 + i), at_chip(step, 1))
                )
            for distance in near_first:
                count = early_rows(hops_of(distance))
                if count:
                    rows = pl.ds(0, count)
                    target = whole.at[2 * place_static(ring - distance, ring) + c, t, rows]
                    z_copies[distance] = [
                        remote(
                            whole.at[c, t, rows], target,
                            z_sems, (parity, 0, distance - 1), at_sector(distance, 0),
                        ),
                        remote(
                            other.at[rows], target,
                            z_sems, (parity, 1, distance - 1), at_sector(distance, 1),
                        ),
                    ]
            scalar_copies = send_scalars(k - 1, values()) if k else send_environments()

            def turn():
                for copy in own_copies:
                    copy.wait_recv()
                for distance in near_first:
                    count = early_rows(hops_of(distance))
                    if count < strip:
                        rows = pl.ds(count, strip - count)
                        late_copies[distance] = remote(
                            whole.at[pl.ds(0, 2), :, rows],
                            whole.at[pl.ds(2 * place_static(ring - distance, ring), 2), :, rows],
                            late_sems, (parity, distance - 1), at_sector(distance, 0),
                        )

            for index in range(2, n_chunks):
                if index == turn_at:
                    turn()
                for distance in members(index):
                    for copy in z_copies[distance]:
                        copy.wait_recv()
                first, count = chunks[index]
                rows = pl.ds(0, early_rows(hops_of(members(index)[0])))
                piece = whole.at[pl.ds(2 * first, 2 * count), t, rows]
                for i, step in enumerate(term_steps):
                    x_copies[index, i] = remote(piece, piece, x_sems, (parity, i, index), at_term(step))
            if k:
                scalar_copies = pass_scalars(k - 1, scalar_copies)
            for copy in before:
                copy.wait_send()
            for index in range(1, n_chunks):
                if k and index == n_chunks - 1:
                    use_totals(take_scalars(k - 1, scalar_copies, 3))
                for distance in members(index):
                    if distance in late_copies:
                        late_copies[distance].wait_recv()
                if index > 1:
                    for i in range(len(term_steps)):
                        x_copies[index, i].wait_recv()
            sent = own_copies + list(late_copies.values()) + list(x_copies.values())
            return sent + [copy for pair in z_copies.values() for copy in pair]

        def sector_place(sector):
            return 2 * place(wrap(sector // 2 - z + ring, ring), ring) + sector % 2

        def apply_terms(whole, send=None):
            for turn_of in range(2):
                s = wrap(c + 1 - turn_of, 2)
                for w in range(terms):
                    spots = [sector_place(sources[s, i, 0, w]) for i in range(couplings)]
                    weights = [sixj_table[sixj_index[s, i, 0, w]] for i in range(couplings)]
                    for q in range(terms_axis):
                        total = weights[0] * whole[spots[0], q].astype(F32)
                        for i in range(1, couplings):
                            total = total + weights[i] * whole[spots[i], q].astype(F32)
                        mixed[turn_of, w, pl.ds(q * strip, strip), :] = total.astype(BF16)
                    product = jnp.dot(mixed[turn_of, w], right[s, w], preferred_element_type=F32)
                    right_part[turn_of, w // 2, pl.ds(w % 2 * half, half), :] = product.astype(BF16)
                total = None
                for p in range(terms // 2):
                    both = jnp.concatenate([left[s, 2 * p], left[s, 2 * p + 1]], axis=1)
                    product = jnp.dot(both, right_part[turn_of, p], preferred_element_type=F32)
                    total = product if total is None else total + product
                part[turn_of] = total
                if send is not None:
                    send(turn_of)

        def image_of(k, whole):
            copies = []

            def send(turn_of):
                outgoing[turn_of] = part[turn_of].astype(BF16).reshape(2, terms_axis, strip, width)
                for i, (dt, dc) in enumerate(chip_steps):
                    if dc == 1 - turn_of:
                        copies.append(
                            remote(
                                outgoing.at[turn_of, :, wrap(t + dt, terms_axis)], arrived.at[k, i],
                                rs_sems, (k % 2, i), at_chip(dt, dc),
                            )
                        )

            apply_terms(whole, send)
            total = my_strips(part.at[1])
            for copy in copies:
                copy.wait()
            for i in range(len(chip_steps)):
                total = total + arrived[k, i].astype(F32).reshape(quarter, width)
            return total * mask

        def corrected(k, totals, shift):
            norm, cross, square = totals
            delta = 1.0 - cross / norm
            grown = square + 2.0 * delta * cross + delta * delta * norm
            if k == 0:
                scale = lax.rsqrt(norm / volume + EPSILON)
                sigma = scale * lax.rsqrt(scale * scale * (grown / volume) + EPSILON)
            else:
                sigma = lax.rsqrt(grown / volume + EPSILON)
            state = sigma * (next_ref[...] + delta * state_ref[...])
            state_ref[...] = state
            return delta, sigma, shift + delta, state

        sibling = at_sector(0, 1)
        other_columns = pl.ds(pl.multiple_of((1 - c) * half, half), half)
        pair_copies = [
            remote(sources_hbm, sources.at[c], pair_sems, (0,), sibling),
            remote(index_hbm, sixj_index.at[c], pair_sems, (1,), sibling),
        ]

        def send_environments():
            load_right.wait()
            pair_copies.append(remote(right.at[c], right.at[c], pair_sems, (2,), sibling))
            load_whole.wait()
            pair_copies.append(
                remote(left_whole.at[:, :, other_columns], left.at[c], pair_sems, (3,), sibling)
            )
            pair_copies.append(remote(left_whole, previous, left_sems, (), at_segment(1, 0)))
            load_left.wait()

        known = {"shift": jnp.zeros((1, 1), F32)}

        def step_totals(k):
            def use(totals):
                known["delta"], known["sigma"], known["shift"], _ = corrected(k, totals, known["shift"])

            return use

        values, sent = None, []
        for k in range(ITERS):
            sent = gather(k, values, step_totals(k - 1), sent)
            if k == 0:
                for copy in pair_copies[0:4]:
                    copy.wait()
            image = image_of(k, gathered[k])
            if k:
                image = known["sigma"] * (image + known["delta"] * image_ref[...])
            image_ref[...] = image
            state = state_ref[...]
            following = (1.0 + known["shift"]) * state - STEP * image
            next_ref[...] = following
            stage(k + 1, following)

            def values(state=state, following=following):
                return [fold(state * state), fold(following * state), fold(following * following)]


        block_copies, onward = [], []

        def last_totals(totals):
            known["delta"], known["sigma"], _, state = corrected(ITERS - 1, totals, known["shift"])
            block[c, :, t] = state.astype(BF16).reshape(2, strip, width)
            mine = block.at[c, :, t]
            for i, (dt, dc) in enumerate(chip_steps):
                block_copies.append(remote(mine, mine, sol_sems, (i,), at_chip(dt, dc)))
            for dt in range(terms_axis):
                onward.append(
                    remote(mine, previous_block.at[:, t], sol_y_sems, (dt,), at_segment(1, dt))
                )

        sent = gather(ITERS, values, last_totals, sent)
        apply_terms(gathered[ITERS])
        for copy in block_copies:
            copy.wait()
        solved[...] = block[c].reshape(width, width)
        solved_copy = pltpu.make_async_copy(solved, solution_out.at[0, 0], load_sem.at[0])
        solved_copy.start()
        state = state_ref[...]
        overlap = part[0] * block[1 - c].reshape(width, width).astype(F32)
        overlap = fold(overlap + part[1] * block[c].reshape(width, width).astype(F32))
        overlap = known["sigma"] * (overlap + known["delta"] * fold(state * image_ref[...]))
        energy_copies = send_scalars(ITERS, [fold(state * state), overlap])
        for copy in sent:
            copy.wait_send()

        pair_copies[4].wait()
        for copy in onward:
            copy.wait()

        @pl.when(y == 0)
        def _():
            copy = pltpu.make_async_copy(left_whole, handoff_out.at[0, :, 0], load_sem.at[1])
            copy.start()
            copy.wait()

        @pl.when(y != 0)
        def _():
            received = previous_block[...].reshape(width, width)
            turned[...] = received.T
            for w in range(terms):
                inner = jnp.dot(previous[w], received, preferred_element_type=F32)
                right_part[w % 2, w // 2] = inner.astype(BF16)
            for w in range(terms):
                fresh = jnp.dot(turned[...], right_part[w % 2, w // 2], preferred_element_type=F32)
                previous[w] = (fresh * (1.0 / width**0.5)).astype(BF16)
            copy = pltpu.make_async_copy(previous, handoff_out.at[0, :, 0], load_sem.at[1])
            copy.start()
            copy.wait()

        energy_copies = pass_scalars(ITERS, energy_copies)
        norm, overlap = take_scalars(ITERS, energy_copies, 2)
        solved_copy.wait()
        energy_out[...] = jnp.broadcast_to(overlap / norm, (1, 128))

    square = (width, width)
    vmem = pl.BlockSpec(memory_space=pltpu.VMEM)
    smem = pltpu.SMEM
    held = pl.BlockSpec(memory_space=pl.ANY)
    others = terms_axis - 1
    peers = 2 * terms_axis - 1
    dma = pltpu.SemaphoreType.DMA
    return pl.pallas_call(
        kernel,
        out_shape=(
            jax.ShapeDtypeStruct((1, 1) + square, BF16),
            jax.ShapeDtypeStruct((1, 128), F32),
            jax.ShapeDtypeStruct((1, terms, 1) + square, BF16),
        ),
        in_specs=[held] * 7,
        out_specs=(held, vmem, held),
        scratch_shapes=[
            pltpu.VMEM(square, F32),
            smem((1,), jnp.int32),
            smem((2, couplings, 1, terms), jnp.int32),
            smem((2, couplings, 1, terms), jnp.int32),
            smem((levels,), F32),
            pltpu.VMEM((terms,) + square, BF16),
            pltpu.VMEM((2, terms, width, half), BF16),
            pltpu.VMEM((2, terms) + square, BF16),
            pltpu.VMEM((terms,) + square, BF16),
        ]
        + [pltpu.VMEM((sectors, terms_axis, strip, width), BF16)] * gathers
        + [
            pltpu.VMEM((gathers, strip, width), BF16),
            pltpu.VMEM((2, terms, half, width), BF16),
            pltpu.VMEM((2, terms // 2) + square, BF16),
            pltpu.VMEM((2,) + square, F32),
            pltpu.VMEM((2, 2, terms_axis, strip, width), BF16),
            pltpu.VMEM((ITERS, peers, 2, strip, width), BF16),
            pltpu.VMEM(square, BF16),
            pltpu.VMEM(square, BF16),
            pltpu.VMEM((quarter, width), F32),
            pltpu.VMEM((quarter, width), F32),
            pltpu.VMEM((quarter, width), F32),
            pltpu.VMEM((gathers, sectors, 1, 128), F32),
            pltpu.VMEM((gathers, terms_axis, 1, 128), F32),
            pltpu.VMEM((2, 2, terms_axis, strip, width), BF16),
            pltpu.VMEM((2, terms_axis, strip, width), BF16),
            dma((8,)),
            dma((2,)),
            dma((2, 4)),
            dma((2, 2, 2, ring - 1)),
            dma((2, 2, ring - 1)),
            dma((2, 2, 2, terms_axis)),
            dma((2, 2, others, n_chunks)),
            dma((2, 2, peers)),
            dma((2, 2, sectors - 1)),
            dma((2, 2, others)),
            dma((2, peers)),
            dma((2, terms_axis)),
        ],
        compiler_params=pltpu.CompilerParams(
            collective_id=1, has_side_effects=True, vmem_limit_bytes=56500 * 1024
        ),
    )


def hand_over(state, energy, handoff):
    terms = handoff.shape[1]

    def kernel(state_in, energy_in, handoff_in, state_out, energy_out, handoff_out, a, b, c, sems):
        moves = [(state_in, a, state_out), (energy_in, b, energy_out)] + [
            (handoff_in.at[0, w], c.at[0, w], handoff_out.at[0, w]) for w in range(terms)
        ]
        loads = [pltpu.make_async_copy(m[0], m[1], sems.at[0, i]) for i, m in enumerate(moves)]
        stores = [pltpu.make_async_copy(m[1], m[2], sems.at[1, i]) for i, m in enumerate(moves)]
        for copy in loads:
            copy.start()
        for load, store in zip(loads, stores):
            load.wait()
            store.start()
        for copy in stores:
            copy.wait()

    held = pl.BlockSpec(memory_space=pl.ANY)
    arrays = (state, energy, handoff)
    return pl.pallas_call(
        kernel,
        out_shape=tuple(jax.ShapeDtypeStruct(array.shape, array.dtype) for array in arrays),
        in_specs=[held] * 3,
        out_specs=(held,) * 3,
        scratch_shapes=[pltpu.VMEM(array.shape, array.dtype) for array in arrays]
        + [pltpu.SemaphoreType.DMA((2, terms + 2))],
        compiler_params=pltpu.CompilerParams(vmem_limit_bytes=56500 * 1024),
    )(*arrays)


def solution(mesh):
    def local(two_site, left_env, right_env, block_dims, sources, sixj_index, sixj_table):
        call = build(
            mesh.shape["chain"], mesh.shape["sector"], mesh.shape["term"],
            left_env.shape[1], sources.shape[2], sixj_table.shape[0], two_site.shape[2],
        )
        state, energy, handoff = call(
            two_site, left_env, right_env, block_dims, sources.transpose(2, 1, 0),
            sixj_index.transpose(2, 1, 0), sixj_table
        )
        state, energy, handoff = hand_over(state, energy, handoff)
        return state, energy[0, 0:1], handoff

    return jax.shard_map(
        local,
        mesh=mesh,
        in_specs=(
            P("chain", "sector", None, None),
            P("chain", "term", "sector", None, None),
            P("chain", "term", "sector", None, None),
            P("sector"),
            P("term", "sector", None),
            P("term", "sector", None),
            P(),
        ),
        out_specs=(
            P("chain", "sector", None, None),
            P("chain"),
            P("chain", "term", "sector", None, None),
        ),
        check_vma=False,
    )
```

```python
import jax
import jax.numpy as jnp
from jax import lax
from jax.experimental import pallas as pl
from jax.experimental.pallas import tpu as pltpu
from jax.sharding import PartitionSpec as P

ITERS = 4
STEP = 0.1
EPSILON = 1e-06
MESH = pl.DeviceIdType.MESH
F32 = jnp.float32
BF16 = jnp.bfloat16


def place(distance, ring):
    half = ring // 2
    return jnp.where(
        distance == 0,
        0,
        jnp.where(
            distance < half,
            2 * distance - 1,
            jnp.where(distance == half, ring - 1, 2 * (ring - distance)),
        ),
    )


def place_static(distance, ring):
    half = ring // 2
    if distance == 0:
        return 0
    if distance < half:
        return 2 * distance - 1
    return ring - 1 if distance == half else 2 * (ring - distance)


def build(segments, sectors, terms_axis, terms, couplings, levels, width):
    ring = sectors // 2
    half = width // 2
    strip = half // terms_axis
    quarter = 2 * strip
    gathers = ITERS + 1
    volume = float(sectors * width * width)
    chunks = [(0, 1)]
    for reach in range(1, ring // 2):
        chunks.append((2 * reach - 1, 2))
    chunks.append((ring - 1, 1))
    near_first = sorted(range(1, ring), key=lambda d: place_static(d, ring))
    late = 16
    turn_at = 2
    n_chunks = len(chunks)

    def kernel(
        two_site_hbm, left_hbm, right_hbm, dims_hbm, sources_hbm, index_hbm, table_hbm,
        solution_out, energy_out, handoff_out,
        two_site, dims, sources, sixj_index, sixj_table, left_whole, left, right, previous, g0, g1, g2, g3, g4,
        other_half, mixed, right_part, part, outgoing, arrived, turned, solved,
        state_ref, image_ref, next_ref, scalars, scalars_term, block, previous_block,
        load_sem, left_sems, pair_sems, z_sems, late_sems, own_sems, x_sems, rs_sems, sz_sems, sx_sems, sol_sems, sol_y_sems,
    ):
        gathered = (g0, g1, g2, g3, g4)
        y = lax.axis_index("chain")
        b = lax.axis_index("sector")
        t = lax.axis_index("term")
        z = b // 2
        c = b % 2

        def wrap(value, count):
            return lax.rem(value + count, count)

        def at_term(step):
            return (y, b, wrap(t + step, terms_axis))

        def at_sector(dz, dc):
            return (y, wrap(z + dz, ring) * 2 + wrap(c + dc, 2), t)

        def at_segment(dy, dt):
            return (wrap(y + dy, segments), b, wrap(t + dt, terms_axis))

        term_steps = (1, terms_axis - 1) + tuple(range(2, terms_axis - 1))
        sector_steps = [(dz, dc) for dz in range(ring) for dc in range(2) if (dz, dc) != (0, 0)]
        chip_steps = [
            (dt, dc) for dc in range(2) for dt in (0,) + term_steps if (dt, dc) != (0, 0)
        ]

        def at_chip(dt, dc):
            return (y, z * 2 + wrap(c + dc, 2), wrap(t + dt, terms_axis))

        def my_strips(ref):
            low = ref[pl.ds(pl.multiple_of(t * strip, strip), strip), :]
            high = ref[pl.ds(pl.multiple_of(half + t * strip, strip), strip), :]
            return jnp.concatenate([low, high], axis=0)

        def left_half(core):
            return left_hbm.at[0, :, 0, :, pl.ds(pl.multiple_of(core * half, half), half)]

        load_whole = pltpu.make_async_copy(left_hbm.at[0, :, 0], left_whole, load_sem.at[7])
        load_left = pltpu.make_async_copy(left_half(c), left.at[c], load_sem.at[0])
        load_right = pltpu.make_async_copy(right_hbm.at[0, :, 0], right.at[c], load_sem.at[1])
        small = [
            pltpu.make_async_copy(source, target, load_sem.at[2 + i])
            for i, (source, target) in enumerate([
                (two_site_hbm.at[0, 0], two_site), (dims_hbm, dims), (sources_hbm, sources.at[c]),
                (index_hbm, sixj_index.at[c]), (table_hbm, sixj_table),
            ])
        ]
        for copy in small:
            copy.start()
        load_right.start()
        load_whole.start()
        load_left.start()

        barrier = pltpu.get_barrier_semaphore()
        for step in term_steps:
            for dc in range(2):
                pl.semaphore_signal(barrier, inc=1, device_id=at_chip(step, dc), device_id_type=MESH)
        for dz, dc in sector_steps:
            pl.semaphore_signal(barrier, inc=1, device_id=at_sector(dz, dc), device_id_type=MESH)
        for dt in range(terms_axis):
            pl.semaphore_signal(barrier, inc=1, device_id=at_segment(-1, dt), device_id_type=MESH)

        def remote(source, target, sems, index, device):
            copy = pltpu.make_async_remote_copy(
                src_ref=source,
                dst_ref=target,
                send_sem=sems.at[(0,) + index],
                recv_sem=sems.at[(1,) + index],
                device_id=device,
                device_id_type=MESH,
            )
            copy.start()
            return copy

        for copy in small:
            copy.wait()
        limit = dims[0]
        row_ids = lax.broadcasted_iota(jnp.int32, (quarter, width), 0)
        row_ids = t * strip + jnp.where(row_ids < strip, row_ids, row_ids - strip + half)
        column_ids = lax.broadcasted_iota(jnp.int32, (quarter, width), 1)
        mask = jnp.where((row_ids < limit) & (column_ids < limit), 1.0, 0.0).astype(F32)

        def stage(k, value):
            low, high = value[0:strip], value[strip:quarter]
            gathered[k][c, t] = jnp.where(c == 0, low, high).astype(BF16)
            other_half[k] = jnp.where(c == 0, high, low).astype(BF16)

        state = my_strips(two_site) * mask
        state_ref[...] = state
        stage(0, state)

        pl.semaphore_wait(barrier, 2 * len(term_steps) + len(sector_steps) + terms_axis)

        lanes = lax.broadcasted_iota(jnp.int32, (1, 128), 1)

        def fold(value):
            return jnp.sum(jnp.sum(value, axis=0, keepdims=True), axis=1, keepdims=True)

        def send_scalars(k, values):
            packed = jnp.zeros((1, 128), F32)
            for i, value in enumerate(values):
                packed = jnp.where(lanes == i, value, packed)
            scalars[k, b] = packed
            return [
                remote(scalars.at[k, b], scalars.at[k, b], sz_sems, (k % 2, i), at_sector(dz, dc))
                for i, (dz, dc) in enumerate(sector_steps)
            ]

        def pass_scalars(k, copies):
            for copy in copies:
                copy.wait()
            scalars_term[k, t] = jnp.sum(scalars[k], axis=0)
            return [
                remote(scalars_term.at[k, t], scalars_term.at[k, t], sx_sems, (k % 2, i), at_term(step))
                for i, step in enumerate(term_steps)
            ]

        def take_scalars(k, copies, count):
            for copy in copies:
                copy.wait()
            total = jnp.sum(scalars_term[k], axis=0)
            return [
                jnp.sum(jnp.where(lanes == i, total, 0.0), axis=1, keepdims=True) for i in range(count)
            ]

        def gather(k, values, use_totals, before):
            whole = gathered[k]
            other = other_half.at[k]
            parity = k % 2
            x_copies, z_copies, late_copies = {}, {}, {}

            def early_rows(hops):
                return {1: 0, 2: strip - late}.get(hops, strip)

            def hops_of(distance):
                return min(distance, ring - distance)

            def members(index):
                first, count = chunks[index]
                return [
                    d for d in range(1, ring) if first <= place_static(ring - d, ring) < first + count
                ]

            own_copies = [remote(other, whole.at[c, t], own_sems, (parity, 0, 0), at_sector(0, 1))]
            for i, step in enumerate(term_steps):
                own_copies.append(
                    remote(
                        whole.at[c, t], whole.at[c, t], own_sems, (parity, 0, 1 + i), at_chip(step, 0)
                    )
                )
                own_copies.append(
                    remote(other, whole.at[c, t], own_sems, (parity, 1, 1 + i), at_chip(step, 1))
                )
            for distance in near_first:
                count = early_rows(hops_of(distance))
                if count:
                    rows = pl.ds(0, count)
                    target = whole.at[2 * place_static(ring - distance, ring) + c, t, rows]
                    z_copies[distance] = [
                        remote(
                            whole.at[c, t, rows], target,
                            z_sems, (parity, 0, distance - 1), at_sector(distance, 0),
                        ),
                        remote(
                            other.at[rows], target,
                            z_sems, (parity, 1, distance - 1), at_sector(distance, 1),
                        ),
                    ]
            scalar_copies = send_scalars(k - 1, values()) if k else send_environments()

            def turn():
                for copy in own_copies:
                    copy.wait_recv()
                for distance in near_first:
                    count = early_rows(hops_of(distance))
                    if count < strip:
                        rows = pl.ds(count, strip - count)
                        late_copies[distance] = remote(
                            whole.at[pl.ds(0, 2), :, rows],
                            whole.at[pl.ds(2 * place_static(ring - distance, ring), 2), :, rows],
                            late_sems, (parity, distance - 1), at_sector(distance, 0),
                        )

            for index in range(2, n_chunks):
                if index == turn_at:
                    turn()
                for distance in members(index):
                    for copy in z_copies[distance]:
                        copy.wait_recv()
                first, count = chunks[index]
                rows = pl.ds(0, early_rows(hops_of(members(index)[0])))
                piece = whole.at[pl.ds(2 * first, 2 * count), t, rows]
                for i, step in enumerate(term_steps):
                    x_copies[index, i] = remote(piece, piece, x_sems, (parity, i, index), at_term(step))
            if k:
                scalar_copies = pass_scalars(k - 1, scalar_copies)
            for copy in before:
                copy.wait_send()
            for index in range(1, n_chunks):
                if k == ITERS and index == n_chunks - 1:
                    use_totals(take_scalars(k - 1, scalar_copies, 3))
                for distance in members(index):
                    if distance in late_copies:
                        late_copies[distance].wait_recv()
                if index > 1:
                    for i in range(len(term_steps)):
                        x_copies[index, i].wait_recv()
            if 0 < k < ITERS:
                use_totals(take_scalars(k - 1, scalar_copies, 3))
            sent = own_copies + list(late_copies.values()) + list(x_copies.values())
            return sent + [copy for pair in z_copies.values() for copy in pair]

        def sector_place(sector):
            return 2 * place(wrap(sector // 2 - z + ring, ring), ring) + sector % 2

        def apply_terms(whole, send=None):
            for turn_of in range(2):
                s = wrap(c + 1 - turn_of, 2)
                for w in range(terms):
                    spots = [sector_place(sources[s, i, 0, w]) for i in range(couplings)]
                    weights = [sixj_table[sixj_index[s, i, 0, w]] for i in range(couplings)]
                    for q in range(terms_axis):
                        total = weights[0] * whole[spots[0], q].astype(F32)
                        for i in range(1, couplings):
                            total = total + weights[i] * whole[spots[i], q].astype(F32)
                        mixed[turn_of, w, pl.ds(q * strip, strip), :] = total.astype(BF16)
                    product = jnp.dot(mixed[turn_of, w], right[s, w], preferred_element_type=F32)
                    right_part[turn_of, w // 2, pl.ds(w % 2 * half, half), :] = product.astype(BF16)
                total = None
                for p in range(terms // 2):
                    both = jnp.concatenate([left[s, 2 * p], left[s, 2 * p + 1]], axis=1)
                    product = jnp.dot(both, right_part[turn_of, p], preferred_element_type=F32)
                    total = product if total is None else total + product
                part[turn_of] = total
                if send is not None:
                    send(turn_of)

        def image_of(k, whole):
            copies = []

            def send(turn_of):
                outgoing[turn_of] = part[turn_of].astype(BF16).reshape(2, terms_axis, strip, width)
                for i, (dt, dc) in enumerate(chip_steps):
                    if dc == 1 - turn_of:
                        copies.append(
                            remote(
                                outgoing.at[turn_of, :, wrap(t + dt, terms_axis)], arrived.at[k, i],
                                rs_sems, (k % 2, i), at_chip(dt, dc),
                            )
                        )

            apply_terms(whole, send)
            total = my_strips(part.at[1])
            for copy in copies:
                copy.wait()
            for i in range(len(chip_steps)):
                total = total + arrived[k, i].astype(F32).reshape(quarter, width)
            return total * mask

        def corrected(k, totals, shift):
            norm, cross, square = totals
            delta = 1.0 - cross / norm
            grown = square + 2.0 * delta * cross + delta * delta * norm
            if k == 0:
                scale = lax.rsqrt(norm / volume + EPSILON)
                sigma = scale * lax.rsqrt(scale * scale * (grown / volume) + EPSILON)
            else:
                sigma = lax.rsqrt(grown / volume + EPSILON)
            state = sigma * (next_ref[...] + delta * state_ref[...])
            state_ref[...] = state
            return delta, sigma, shift + delta, state

        sibling = at_sector(0, 1)
        other_columns = pl.ds(pl.multiple_of((1 - c) * half, half), half)
        pair_copies = [
            remote(sources_hbm, sources.at[c], pair_sems, (0,), sibling),
            remote(index_hbm, sixj_index.at[c], pair_sems, (1,), sibling),
        ]

        def send_environments():
            load_right.wait()
            pair_copies.append(remote(right.at[c], right.at[c], pair_sems, (2,), sibling))
            load_whole.wait()
            pair_copies.append(
                remote(left_whole.at[:, :, other_columns], left.at[c], pair_sems, (3,), sibling)
            )
            pair_copies.append(remote(left_whole, previous, left_sems, (), at_segment(1, 0)))
            load_left.wait()

        known = {"shift": jnp.zeros((1, 1), F32)}

        def step_totals(k):
            def use(totals):
                known["delta"], known["sigma"], known["shift"], _ = corrected(k, totals, known["shift"])

            return use

        values, sent = None, []
        for k in range(ITERS):
            sent = gather(k, values, step_totals(k - 1), sent)
            if k == 0:
                for copy in pair_copies[0:4]:
                    copy.wait()
            image = image_of(k, gathered[k])
            if k:
                image = known["sigma"] * (image + known["delta"] * image_ref[...])
            image_ref[...] = image
            state = state_ref[...]
            following = (1.0 + known["shift"]) * state - STEP * image
            next_ref[...] = following
            stage(k + 1, following)

            def values(state=state, following=following):
                return [fold(state * state), fold(following * state), fold(following * following)]


        block_copies, onward = [], []

        def last_totals(totals):
            known["delta"], known["sigma"], _, state = corrected(ITERS - 1, totals, known["shift"])
            block[c, :, t] = state.astype(BF16).reshape(2, strip, width)
            mine = block.at[c, :, t]
            for i, (dt, dc) in enumerate(chip_steps):
                block_copies.append(remote(mine, mine, sol_sems, (i,), at_chip(dt, dc)))
            for dt in range(terms_axis):
                onward.append(
                    remote(mine, previous_block.at[:, t], sol_y_sems, (dt,), at_segment(1, dt))
                )

        sent = gather(ITERS, values, last_totals, sent)
        apply_terms(gathered[ITERS])
        for copy in block_copies:
            copy.wait()
        solved[...] = block[c].reshape(width, width)
        solved_copy = pltpu.make_async_copy(solved, solution_out.at[0, 0], load_sem.at[0])
        solved_copy.start()
        state = state_ref[...]
        overlap = part[0] * block[1 - c].reshape(width, width).astype(F32)
        overlap = fold(overlap + part[1] * block[c].reshape(width, width).astype(F32))
        overlap = known["sigma"] * (overlap + known["delta"] * fold(state * image_ref[...]))
        energy_copies = send_scalars(ITERS, [fold(state * state), overlap])
        for copy in sent:
            copy.wait_send()

        pair_copies[4].wait()
        for copy in onward:
            copy.wait()

        @pl.when(y == 0)
        def _():
            copy = pltpu.make_async_copy(left_whole, handoff_out.at[0, :, 0], load_sem.at[1])
            copy.start()
            copy.wait()

        @pl.when(y != 0)
        def _():
            received = previous_block[...].reshape(width, width)
            turned[...] = received.T
            for w in range(terms):
                inner = jnp.dot(previous[w], received, preferred_element_type=F32)
                right_part[w % 2, w // 2] = inner.astype(BF16)
            for w in range(terms):
                fresh = jnp.dot(turned[...], right_part[w % 2, w // 2], preferred_element_type=F32)
                previous[w] = (fresh * (1.0 / width**0.5)).astype(BF16)
            copy = pltpu.make_async_copy(previous, handoff_out.at[0, :, 0], load_sem.at[1])
            copy.start()
            copy.wait()

        energy_copies = pass_scalars(ITERS, energy_copies)
        norm, overlap = take_scalars(ITERS, energy_copies, 2)
        solved_copy.wait()
        energy_out[...] = jnp.broadcast_to(overlap / norm, (1, 128))

    square = (width, width)
    vmem = pl.BlockSpec(memory_space=pltpu.VMEM)
    smem = pltpu.SMEM
    held = pl.BlockSpec(memory_space=pl.ANY)
    others = terms_axis - 1
    peers = 2 * terms_axis - 1
    dma = pltpu.SemaphoreType.DMA
    return pl.pallas_call(
        kernel,
        out_shape=(
            jax.ShapeDtypeStruct((1, 1) + square, BF16),
            jax.ShapeDtypeStruct((1, 128), F32),
            jax.ShapeDtypeStruct((1, terms, 1) + square, BF16),
        ),
        in_specs=[held] * 7,
        out_specs=(held, vmem, held),
        scratch_shapes=[
            pltpu.VMEM(square, F32),
            smem((1,), jnp.int32),
            smem((2, couplings, 1, terms), jnp.int32),
            smem((2, couplings, 1, terms), jnp.int32),
            smem((levels,), F32),
            pltpu.VMEM((terms,) + square, BF16),
            pltpu.VMEM((2, terms, width, half), BF16),
            pltpu.VMEM((2, terms) + square, BF16),
            pltpu.VMEM((terms,) + square, BF16),
        ]
        + [pltpu.VMEM((sectors, terms_axis, strip, width), BF16)] * gathers
        + [
            pltpu.VMEM((gathers, strip, width), BF16),
            pltpu.VMEM((2, terms, half, width), BF16),
            pltpu.VMEM((2, terms // 2) + square, BF16),
            pltpu.VMEM((2,) + square, F32),
            pltpu.VMEM((2, 2, terms_axis, strip, width), BF16),
            pltpu.VMEM((ITERS, peers, 2, strip, width), BF16),
            pltpu.VMEM(square, BF16),
            pltpu.VMEM(square, BF16),
            pltpu.VMEM((quarter, width), F32),
            pltpu.VMEM((quarter, width), F32),
            pltpu.VMEM((quarter, width), F32),
            pltpu.VMEM((gathers, sectors, 1, 128), F32),
            pltpu.VMEM((gathers, terms_axis, 1, 128), F32),
            pltpu.VMEM((2, 2, terms_axis, strip, width), BF16),
            pltpu.VMEM((2, terms_axis, strip, width), BF16),
            dma((8,)),
            dma((2,)),
            dma((2, 4)),
            dma((2, 2, 2, ring - 1)),
            dma((2, 2, ring - 1)),
            dma((2, 2, 2, terms_axis)),
            dma((2, 2, others, n_chunks)),
            dma((2, 2, peers)),
            dma((2, 2, sectors - 1)),
            dma((2, 2, others)),
            dma((2, peers)),
            dma((2, terms_axis)),
        ],
        compiler_params=pltpu.CompilerParams(
            collective_id=1, has_side_effects=True, vmem_limit_bytes=56500 * 1024
        ),
    )


def hand_over(state, energy, handoff):
    terms = handoff.shape[1]

    def kernel(state_in, energy_in, handoff_in, state_out, energy_out, handoff_out, a, b, c, sems):
        moves = [(state_in, a, state_out), (energy_in, b, energy_out)] + [
            (handoff_in.at[0, w], c.at[0, w], handoff_out.at[0, w]) for w in range(terms)
        ]
        loads = [pltpu.make_async_copy(m[0], m[1], sems.at[0, i]) for i, m in enumerate(moves)]
        stores = [pltpu.make_async_copy(m[1], m[2], sems.at[1, i]) for i, m in enumerate(moves)]
        for copy in loads:
            copy.start()
        for load, store in zip(loads, stores):
            load.wait()
            store.start()
        for copy in stores:
            copy.wait()

    held = pl.BlockSpec(memory_space=pl.ANY)
    arrays = (state, energy, handoff)
    return pl.pallas_call(
        kernel,
        out_shape=tuple(jax.ShapeDtypeStruct(array.shape, array.dtype) for array in arrays),
        in_specs=[held] * 3,
        out_specs=(held,) * 3,
        scratch_shapes=[pltpu.VMEM(array.shape, array.dtype) for array in arrays]
        + [pltpu.SemaphoreType.DMA((2, terms + 2))],
        compiler_params=pltpu.CompilerParams(vmem_limit_bytes=56500 * 1024),
    )(*arrays)


def solution(mesh):
    def local(two_site, left_env, right_env, block_dims, sources, sixj_index, sixj_table):
        call = build(
            mesh.shape["chain"], mesh.shape["sector"], mesh.shape["term"],
            left_env.shape[1], sources.shape[2], sixj_table.shape[0], two_site.shape[2],
        )
        state, energy, handoff = call(
            two_site, left_env, right_env, block_dims, sources.transpose(2, 1, 0),
            sixj_index.transpose(2, 1, 0), sixj_table
        )
        state, energy, handoff = hand_over(state, energy, handoff)
        return state, energy[0, 0:1], handoff

    return jax.shard_map(
        local,
        mesh=mesh,
        in_specs=(
            P("chain", "sector", None, None),
            P("chain", "term", "sector", None, None),
            P("chain", "term", "sector", None, None),
            P("sector"),
            P("term", "sector", None),
            P("term", "sector", None),
            P(),
        ),
        out_specs=(
            P("chain", "sector", None, None),
            P("chain"),
            P("chain", "term", "sector", None, None),
        ),
        check_vma=False,
    )
```
